256 devices in a mesh: slab: 64 (over z, x, core), blk: 4 (over y).
Axes of the slice: x: 4, y: 4, z: 8, core: 2. Of those that a mesh axis runs over, the one named last changes fastest.
Arguments:
- volume: bfloat16 [64, 12, 48, 2, 4096], P('slab', 'blk'), may hold values from -6 to 6
- tissue: int32 [64, 12], P('slab', 'blk'), may hold values from 0 to 1
- face_owner: int32 [2, 12, 2, 1], P(None, 'blk'), may hold values from 0 to 3; in each aligned block of 6 rows (0 to 5, 6 to 11, ..., all dimensions but the last counted through in order) at most 3 rows name the same one
- face_slot: int32 [2, 12, 2], P(None, 'blk'), may hold values from 0 to 2
- plane_weight: bfloat16 [48, 432], replicated, may hold values from -0.3125 to 0.3125
- depth_weight: bfloat16 [48, 144], replicated, may hold values from -0.5 to 0.5
- norm_gain: float32 [48], replicated, may hold values from 0.5 to 1.5
- norm_bias: float32 [48], replicated, may hold values from -3 to 3
Outputs:
- features_out: bfloat16 [64, 12, 48, 2, 4096], P('slab', 'blk')
The draws below stay inside these ranges and needn't reach their ends.
Inputs may be any that keep to these rules, and one draw needn't show every extreme that they name: `face_owner`: among the (6) entries of one device for one orientation (its blocks, both sides), no device is named more than 3 times, and in every draw some device is named exactly 3 times.
All inputs are finite; a program needn't handle non-finite values.
Results may differ from the reference program's by a relative error of at most 0.005.
Values may be sent and summed in bfloat16 or wider, within the bound.
No kernel may reach another device: no remote copies, remote signals or barrier semaphores. Data moves between devices by JAX's collectives and lax.ppermute only.
A program may use at most 128 MiB of HBM per device.

```python
import math
import jax
import jax.numpy as jnp
import numpy as np
from jax import lax

C = 48
BZ = 2
BY = 64
BX = 64
SLOTS = 3
SLABS = 64
BLOCKS = 12
CAP = 3
N_BLK = 4


def draw_tissue(key, part):
    key = jax.random.fold_in(key, 11)
    rate_key, roll_key = jax.random.split(key)
    rate = jax.random.randint(rate_key, (SLABS, N_BLK, 1), 3, 11)
    roll = jax.random.randint(roll_key, (SLABS, N_BLK, SLOTS), 0, 10)
    return (roll < rate).astype(jnp.int32).reshape(SLABS, BLOCKS)


def plant(array, rng, least, top_value):
    index_at = [jax.random.randint(jax.random.fold_in(rng, axis), (), 0, length) for axis, length in enumerate(array.shape)]
    main_axis = array.shape.index(max(array.shape))
    next_to = index_at[:main_axis] + [(index_at[main_axis] + 1) % array.shape[main_axis]] + index_at[main_axis + 1:]
    return array.at[tuple(index_at)].set(least).at[tuple(next_to)].set(top_value)


def levels(stream_key, dims, cuts, smallest, largest):
    factor_of = 1.0
    for axis_at, blocks in cuts:
        draws = jax.random.uniform(jax.random.fold_in(jax.random.fold_in(stream_key, 6), axis_at), (blocks,), jnp.float32, smallest / len(cuts), largest / len(cuts))
        factor_of = factor_of * jnp.repeat(jnp.exp(draws), dims[axis_at] // blocks).reshape((-1,) + (1,) * (len(dims) - 1 - axis_at))
    return factor_of


def shared_out(stream_key, own, number, rows, number_of, top, most, skew):
    ranking = jax.random.permutation(stream_key, number_of)
    packed, ordinary = portions_of(number_of, rows * top, most, skew, True), portions_of(number_of, rows * top, most, skew, False)
    places = jnp.arange(number_of)

    def named(lengths, turn):
        used = int((lengths > 0).sum())
        fixed = max(1, used // 4)
        shifted = fixed + (places - fixed + turn * (used - fixed)) % max(1, number_of - fixed)
        return jnp.zeros((number_of,), jnp.int32).at[ranking[jnp.where(places < fixed, places, shifted)]].set(jnp.asarray(lengths, jnp.int32))

    lengths = jnp.where(number % 4 == 0, named(packed, number // 4), named(ordinary, number - number // 4 - 1))
    mixed = jax.random.permutation(jax.random.fold_in(own, 3), number_of)
    donor, sink = mixed[0:number_of // 2 * 2:2], mixed[1:number_of // 2 * 2:2]
    room = jnp.minimum(lengths[donor] - 1, most - lengths[sink]) // 2
    room = jnp.where((donor == ranking[0]) | (sink == ranking[0]) | (lengths[sink] == 0), 0, jnp.maximum(room, 0))
    shifted = jax.random.randint(jax.random.fold_in(own, 4), (number_of // 2,), 0, 1 << 20) % (room + 1)
    lengths = lengths.at[donor].add(-shifted).at[sink].add(shifted)
    labels = jnp.searchsorted(jnp.cumsum(lengths), jnp.arange(rows * top), side="right").astype(jnp.int32)
    grid = labels.reshape(top, rows).T
    grid = grid[jax.random.permutation(jax.random.fold_in(own, 1), rows)]
    turn = jax.random.randint(jax.random.fold_in(own, 2), (rows, 1), 0, top)
    return jnp.take_along_axis(grid, (jnp.arange(top)[None, :] + turn) % top, axis=1)


def portions_of(number_of, total, bound, slope, full):
    loads = [(1 << 20) // math.isqrt(standing ** slope) + 1 for standing in range(1, number_of + 1)]
    largest = bound if full else min(bound, max(-(-total // number_of), total * loads[0] // sum(loads)))
    least = 1 if total - largest >= number_of - 1 else 0
    holding, rest = [largest] + [least] * (number_of - 1), total - largest - least * (number_of - 1)
    while rest > 0:
        free = [i for i in range(1, number_of) if holding[i] < largest] or [i for i in range(1, number_of) if holding[i] < bound]
        mass, remaining = sum([loads[i] for i in free]), rest
        for i in free:
            extra = min(bound - holding[i], max(1, remaining * loads[i] // mass), rest)
            holding[i] = holding[i] + extra
            rest = rest - extra
    return np.array(holding)


def gaussian(key, dims, scale, most, pieces=(), kind=jnp.bfloat16):
    gain = levels(key, dims, pieces, -0.22, 0.18) if pieces else 1.0
    values = jax.random.normal(key, dims, jnp.float32) * scale * gain
    return jnp.minimum(jnp.maximum(values, -most), most).astype(kind)


def setup_inputs(seed: int = 0) -> dict:
    arg_keys = jax.random.split(jax.random.key(seed), 9)
    volume = gaussian(arg_keys[0], (SLABS, BLOCKS, C, BZ, BY * BX), 1.0, 6.0, ((0, 64), (1, 4)))
    tissue = draw_tissue(jax.random.fold_in(arg_keys[8], 71), 0)
    face_owner_keys = jax.random.split(jax.random.fold_in(arg_keys[2], 1), 2 * BLOCKS * 2 // (2 * SLOTS))
    face_owner_turns = jax.random.permutation(jax.random.fold_in(arg_keys[2], 3), 2 * BLOCKS * 2 // (2 * SLOTS))
    face_owner = jax.vmap(lambda own, number: shared_out(jax.random.fold_in(arg_keys[2], 2), own, number, 2 * SLOTS, N_BLK, 1, CAP, 1))(face_owner_keys, face_owner_turns).reshape((2, BLOCKS, 2, 1))
    face_slot = plant(jax.random.randint(arg_keys[3], (2, BLOCKS, 2), 0, SLOTS), jax.random.fold_in(arg_keys[3], 1), 0, SLOTS - 1).astype(jnp.int32)
    plane_weight = gaussian(arg_keys[4], (C, 9 * C), (9 * C) ** -0.5, 0.3125)
    depth_weight = gaussian(arg_keys[5], (C, 3 * C), (3 * C) ** -0.5, 0.5)
    norm_gain = jnp.clip(jax.random.uniform(arg_keys[6], (C,), jnp.float32, 0.5, 1.5), 0.5, 1.5)
    norm_bias = gaussian(arg_keys[7], (C,), 0.5, 3.0, (), jnp.float32)
    return dict(volume=volume, tissue=tissue, face_owner=face_owner, face_slot=face_slot, plane_weight=plane_weight, depth_weight=depth_weight, norm_gain=norm_gain, norm_bias=norm_bias)


def plane_conv(cells_in, north_row, south_row, west_col, east_col, weight):
    channels, layers, row_count, col_count = cells_in.shape
    stacked = jnp.concatenate([north_row[:, :, None, :], cells_in, south_row[:, :, None, :]], axis=2)
    zero_cell = jnp.zeros((channels, layers, 1), cells_in.dtype)
    west_ext = jnp.concatenate([zero_cell, west_col, zero_cell], axis=2)
    east_ext = jnp.concatenate([zero_cell, east_col, zero_cell], axis=2)
    tap_list = []
    for offset in range(3):
        band_rows = stacked[:, :, offset:offset + row_count, :]
        west_band = west_ext[:, :, offset:offset + row_count]
        east_band = east_ext[:, :, offset:offset + row_count]
        tap_list.append(jnp.concatenate([west_band[..., None], band_rows[..., :-1]], axis=3))
        tap_list.append(band_rows)
        tap_list.append(jnp.concatenate([band_rows[..., 1:], east_band[..., None]], axis=3))
    tap_stack = jnp.stack(tap_list, 0).reshape(9 * channels, layers * row_count * col_count)
    return jnp.dot(weight, tap_stack, preferred_element_type=jnp.float32)

def activate(plane_out, gain_vec, bias_vec, live_weight):
    center = lax.optimization_barrier(jnp.mean(plane_out, axis=1, keepdims=True))
    spread = lax.optimization_barrier(jnp.mean(jnp.square(plane_out - center), axis=1, keepdims=True))
    scaled = (plane_out - center) * lax.rsqrt(spread + 1e-05) * gain_vec[:, None] + bias_vec[:, None]
    return (jax.nn.relu(scaled) * live_weight).astype(jnp.bfloat16)

def reference(volume, tissue, face_owner, face_slot, plane_weight, depth_weight, norm_gain, norm_bias):
    volume_cells = volume.reshape(SLABS, BLOCKS, C, BZ, BY, BX)
    live_mask = tissue.astype(jnp.float32)
    masked = volume_cells * tissue.astype(jnp.bfloat16)[:, :, None, None, None, None]
    partner = (face_owner[..., 0] * SLOTS + face_slot).astype(jnp.int32)

    def one_block(flat_index):
        slab_id = flat_index // BLOCKS
        block_id = flat_index % BLOCKS
        own_block = masked[slab_id, block_id]
        partner_ids = partner[:, block_id, :]
        north_row = masked[slab_id, partner_ids[0, 0]][:, :, BY - 1, :]
        south_row = masked[slab_id, partner_ids[0, 1]][:, :, 0, :]
        west_col = masked[slab_id, partner_ids[1, 0]][:, :, :, BX - 1]
        east_col = masked[slab_id, partner_ids[1, 1]][:, :, :, 0]
        plane_out = plane_conv(own_block, north_row, south_row, west_col, east_col, plane_weight)
        return activate(plane_out, norm_gain, norm_bias, live_mask[slab_id, block_id])
    activated = lax.map(one_block, jnp.arange(SLABS * BLOCKS, dtype=jnp.int32))
    columns = activated.reshape(SLABS, BLOCKS, C, BZ, BY * BX)

    def one_column(block_id):
        stack_z = jnp.transpose(columns[:, block_id], (1, 0, 2, 3)).reshape(C, SLABS * BZ, BY * BX)
        zero_layer = jnp.zeros((C, 1, BY * BX), jnp.bfloat16)
        padded = jnp.concatenate([zero_layer, stack_z, zero_layer], axis=1)
        column_layers = SLABS * BZ
        tap_stack = jnp.stack([padded[:, offset:offset + column_layers] for offset in range(3)], 0)
        tap_stack = tap_stack.reshape(3 * C, column_layers * BY * BX)
        mixed_out = jnp.dot(depth_weight, tap_stack, preferred_element_type=jnp.float32)
        mixed_out = jnp.transpose(mixed_out.reshape(C, SLABS, BZ, BY * BX), (1, 0, 2, 3))
        summed = (volume[:, block_id].astype(jnp.float32) + mixed_out) * live_mask[:, block_id][:, None, None, None]
        return summed.astype(jnp.bfloat16)
    result = lax.map(one_column, jnp.arange(BLOCKS, dtype=jnp.int32))
    return jnp.transpose(result, (1, 0, 2, 3, 4))
```

```python
import functools
import jax
import jax.numpy as jnp
from jax import lax
from jax.sharding import PartitionSpec as P
import jax.experimental.pallas as pl
import jax.experimental.pallas.tpu as pltpu

LANES = 128
BF = jnp.bfloat16
F32 = jnp.float32


def lane_ids(rows):
    return lax.broadcasted_iota(jnp.int32, (rows, LANES), 1)


def roll(x, k):
    return pltpu.roll(x, k % LANES, 1)


def split_kernel(tissue_ref, vol_ref, z0_ref, z1_ref, strip_ref):
    slot = pl.program_id(0)
    c, n = z0_ref.shape[1:]
    x = vol_ref[0, 0].reshape(2 * c, n)
    i = lax.broadcasted_iota(jnp.int32, (2 * c, 2 * c), 0)
    j = lax.broadcasted_iota(jnp.int32, (2 * c, 2 * c), 1)
    order = (j == (i % c) * 2 + i // c).astype(F32).astype(BF)
    d = jnp.dot(order, x, preferred_element_type=F32).astype(BF)
    z0_ref[0] = d[:c]
    z1_ref[0] = d[c:]
    live = jnp.where(tissue_ref[slot] > 0, 1.0, 0.0).astype(BF)
    lane = lane_ids(2 * c)
    tiles = n // LANES
    rows = jnp.where(lane < 64, d[:, :LANES], d[:, n - LANES:])
    within = lane % 64
    cols = jnp.zeros((2 * c, LANES), BF)
    for t in range(tiles):
        tile = d[:, t * LANES:(t + 1) * LANES]
        cols = jnp.where(within == t, roll(tile, t - 63), cols)
        cols = jnp.where(within == 32 + t, roll(tile, 32 + t), cols)
    rows = rows * live
    cols = cols * live
    for z in range(2):
        strip_ref[z, 0, 0] = rows[z * c:(z + 1) * c]
        strip_ref[z, 0, 1] = cols[z * c:(z + 1) * c]


def split(tissue, vol):
    _, s, c, z, n = vol.shape
    grid = pltpu.PrefetchScalarGridSpec(
        num_scalar_prefetch=1, grid=(s,),
        in_specs=[pl.BlockSpec((1, 1, c, z, n), lambda b, t: (0, b, 0, 0, 0))],
        out_specs=[pl.BlockSpec((1, c, n), lambda b, t: (b, 0, 0))] * 2
        + [pl.BlockSpec((2, 1, 2, c, LANES), lambda b, t: (0, b, 0, 0, 0))])
    return pl.pallas_call(
        split_kernel, grid_spec=grid, name="split",
        out_shape=[jax.ShapeDtypeStruct((s, c, n), BF)] * 2
        + [jax.ShapeDtypeStruct((2, s, 2, c, LANES), BF)],
        compiler_params=pltpu.CompilerParams(vmem_limit_bytes=48 * 2**20),
    )(tissue, vol)


def assemble_kernel(owner_ref, slot_ref, me_ref, own_ref, one_ref, two_ref, three_ref, halo_ref, table):
    s = own_ref.shape[1]
    c = own_ref.shape[3]
    for k, ref in enumerate((own_ref, one_ref, two_ref, three_ref)):
        table[k] = ref[...]
    lane = lane_ids(c)
    south = lane < 64
    west = lane % 64 < 32
    me = me_ref[0]

    def pick(t, b, e):
        p = (t * s + b) * 2 + e
        return lax.rem(me - owner_ref[p] + 4, 4), slot_ref[p]

    for b in range(s):
        for t, mask in ((0, south), (1, west)):
            lo, hi = (1, 0) if t == 0 else (0, 1)
            lk, ls = pick(t, b, lo)
            hk, hs = pick(t, b, hi)
            for z in range(2):
                halo_ref[z, b, t] = jnp.where(mask, table[lk, z, ls, t], table[hk, z, hs, t])


def assemble(owner, slot, me, strips):
    shape = strips[0].shape
    vm = pl.BlockSpec(memory_space=pltpu.VMEM)
    sm = pl.BlockSpec(memory_space=pltpu.SMEM)
    return pl.pallas_call(
        assemble_kernel, name="assemble",
        in_specs=[sm] * 3 + [vm] * 4, out_specs=vm,
        out_shape=jax.ShapeDtypeStruct(shape, BF),
        scratch_shapes=[pltpu.VMEM((4,) + shape, BF)],
        compiler_params=pltpu.CompilerParams(vmem_limit_bytes=16 * 2**20),
    )(owner, slot, me, *strips)


def conv_layer(x_at, rows, cols, weight, emit):
    c = rows.shape[0]
    lane = lane_ids(c)
    first = lane % 64 == 0
    last = lane % 64 == 63
    low = lane < 64
    zero = jnp.zeros((c, LANES), BF)
    tiles = 32

    def three(tile, west, east):
        return jnp.concatenate([jnp.where(first, west, roll(tile, 1)), tile,
                                jnp.where(last, east, roll(tile, -1))], axis=0)

    def mix(x3):
        return jnp.dot(weight, x3, preferred_element_type=F32)

    edge = mix(three(rows, zero, zero))
    above, edge_south = edge[:c], edge[2 * c:]
    middle = turned = None
    for pair in range(tiles // 2):
        x3 = []
        for t in (2 * pair, 2 * pair + 1):
            x3.append(three(x_at(t), roll(cols, -t), roll(cols, 31 - t)))
        u = mix(jnp.concatenate(x3, axis=1))
        for h in range(2):
            part = u[:, h * LANES:(h + 1) * LANES]
            turn = roll(above + part[2 * c:], 64)
            t = 2 * pair + h
            if t:
                emit(t - 1, middle + jnp.where(low, turned, turn))
            above, middle, turned = part[:c], part[c:2 * c], turn
    turn = roll(above + edge_south, 64)
    emit(tiles - 1, middle + jnp.where(low, turned, turn))


def own_kernel(tissue_ref, z0_ref, z1_ref, halo_ref, weight_ref, norm_ref, act_ref, stat_ref, plane):
    slot = pl.program_id(0)
    c, n = z0_ref.shape[1:]
    weight = weight_ref[...]
    total = [jnp.zeros((c, LANES), F32)]
    for z, ref in enumerate((z0_ref, z1_ref)):
        def emit(t, value, z=z):
            plane[z, :, t * LANES:(t + 1) * LANES] = value
            total[0] += value
        conv_layer(lambda t, ref=ref: ref[0, :, t * LANES:(t + 1) * LANES],
                   halo_ref[z, 0, 0], halo_ref[z, 0, 1], weight, emit)
    scale = 1.0 / (2 * n)
    mean = jnp.sum(total[0], axis=1, keepdims=True) * scale
    mean_b = jnp.broadcast_to(mean, (c, LANES))
    square = jnp.zeros((c, LANES), F32)
    for z in range(2):
        for t in range(n // LANES):
            dev = plane[z, :, t * LANES:(t + 1) * LANES] - mean_b
            square += dev * dev
    var = jnp.sum(square, axis=1, keepdims=True) * scale
    live = jnp.where(tissue_ref[slot] > 0, 1.0, 0.0)
    gain = lax.rsqrt(var + 1e-05) * norm_ref[:, 0:1] * live
    bias = norm_ref[:, 1:2] * live
    gain_b = jnp.broadcast_to(gain, (c, LANES))
    bias_b = jnp.broadcast_to(bias, (c, LANES))
    for z in range(2):
        for t in range(n // LANES):
            at = slice(t * LANES, (t + 1) * LANES)
            act_ref[0, z * c:(z + 1) * c, at] = jnp.maximum(
                (plane[z, :, at] - mean_b) * gain_b + bias_b, 0.0).astype(BF)
    lane = lane_ids(c)
    stat_ref[0] = jnp.where(lane == 0, mean_b, jnp.where(lane == 1, gain_b, bias_b))


def own_layers(tissue, z0, z1, halo, weight, norm):
    s, c, n = z0.shape
    layer = pl.BlockSpec((1, c, n), lambda b, t: (b, 0, 0))
    grid = pltpu.PrefetchScalarGridSpec(
        num_scalar_prefetch=1, grid=(s,),
        in_specs=[layer, layer,
                  pl.BlockSpec((2, 1, 2, c, LANES), lambda b, t: (0, b, 0, 0, 0)),
                  pl.BlockSpec((3 * c, 3 * c), lambda b, t: (0, 0)),
                  pl.BlockSpec((c, 2), lambda b, t: (0, 0))],
        out_specs=[pl.BlockSpec((1, 2 * c, n), lambda b, t: (b, 0, 0)),
                   pl.BlockSpec((1, c, LANES), lambda b, t: (b, 0, 0))],
        scratch_shapes=[pltpu.VMEM((2, c, n), F32)])
    return pl.pallas_call(
        own_kernel, grid_spec=grid, name="own",
        out_shape=[jax.ShapeDtypeStruct((s, 2 * c, n), BF), jax.ShapeDtypeStruct((s, c, LANES), F32)],
        compiler_params=pltpu.CompilerParams(vmem_limit_bytes=32 * 2**20),
    )(tissue, z0, z1, halo, weight, norm)


def final_kernel(tissue_ref, vol_ref, lo_ref, hi_ref, lo_halo_ref, hi_halo_ref, lo_stat_ref, hi_stat_ref,
                 act_ref, weight_ref, depth_ref, out_ref, stack):
    slot = pl.program_id(0)
    c, n = lo_ref.shape[1:]
    weight = weight_ref[...]
    stack[c:3 * c] = act_ref[0]
    for base, ref, halo, stat in ((0, lo_ref, lo_halo_ref, lo_stat_ref), (3 * c, hi_ref, hi_halo_ref, hi_stat_ref)):
        mean, gain, bias = (jnp.broadcast_to(stat[0, :, k:k + 1], (c, LANES)) for k in range(3))

        def emit(t, value):
            stack[base:base + c, t * LANES:(t + 1) * LANES] = jnp.maximum(
                (value - mean) * gain + bias, 0.0).astype(BF)
        conv_layer(lambda t: ref[0, :, t * LANES:(t + 1) * LANES], halo[0, 0], halo[0, 1], weight, emit)
    live = jnp.where(tissue_ref[slot] > 0, 1.0, 0.0)
    wide = 512
    for t in range(n // wide):
        at = slice(t * wide, (t + 1) * wide)
        mixed = jnp.dot(depth_ref[...], stack[:, at], preferred_element_type=F32)
        given = vol_ref[0, 0, :, :, at].reshape(2 * c, wide).astype(F32)
        out_ref[0, 0, :, :, at] = ((given + mixed) * live).astype(BF).reshape(c, 2, wide)


def final(tissue, vol, lo, hi, lo_halo, hi_halo, lo_stat, hi_stat, act, weight, depth):
    s, c, n = lo.shape
    layer = pl.BlockSpec((1, c, n), lambda b, t: (b, 0, 0))
    halo = pl.BlockSpec((1, 2, c, LANES), lambda b, t: (b, 0, 0, 0))
    stat = pl.BlockSpec((1, c, LANES), lambda b, t: (b, 0, 0))
    whole = pl.BlockSpec((1, 1, c, 2, n), lambda b, t: (0, b, 0, 0, 0))
    grid = pltpu.PrefetchScalarGridSpec(
        num_scalar_prefetch=1, grid=(s,),
        in_specs=[whole, layer, layer, halo, halo, stat, stat,
                  pl.BlockSpec((1, 2 * c, n), lambda b, t: (b, 0, 0)),
                  pl.BlockSpec((3 * c, 3 * c), lambda b, t: (0, 0)),
                  pl.BlockSpec((2 * c, 4 * c), lambda b, t: (0, 0))],
        out_specs=whole,
        scratch_shapes=[pltpu.VMEM((4 * c, n), BF)])
    return pl.pallas_call(
        final_kernel, grid_spec=grid, name="final",
        out_shape=jax.ShapeDtypeStruct(vol.shape, BF),
        compiler_params=pltpu.CompilerParams(vmem_limit_bytes=32 * 2**20),
    )(tissue, vol, lo, hi, lo_halo, hi_halo, lo_stat, hi_stat, act, weight, depth)


def shifted(value, axis, steps):
    count = lax.axis_size(axis)
    first, last = (max(0, -steps), min(count, count - steps))
    return lax.ppermute(value, axis, [(source, source + steps) for source in range(first, last)])


def ring(value, axis, steps):
    count = lax.axis_size(axis)
    return lax.ppermute(value, axis, [(i, (i + steps) % count) for i in range(count)])


def prepare(plane_weight, depth_weight, norm_gain, norm_bias):
    c = plane_weight.shape[0]
    weight = plane_weight.reshape(c, 3, 3 * c).transpose(1, 0, 2).reshape(3 * c, 3 * c)
    pad = jnp.zeros((c, c), depth_weight.dtype)
    depth = jnp.stack([jnp.concatenate([depth_weight, pad], 1),
                       jnp.concatenate([pad, depth_weight], 1)], 1).reshape(2 * c, 4 * c)
    norm = jnp.stack([norm_gain, norm_bias], 1)
    return weight, depth, norm


def body(volume, tissue, face_owner, face_slot, plane_weight, depth_weight, norm_gain, norm_bias):
    live = tissue[0]
    owner = face_owner.reshape(-1)
    slot = face_slot.reshape(-1)
    me = lax.axis_index("blk").reshape(1)
    weight, depth, norm = prepare(plane_weight, depth_weight, norm_gain, norm_bias)
    z0, z1, strips = split(live, volume)
    lo = shifted(z1, "slab", 1)
    hi = shifted(z0, "slab", -1)
    halo = assemble(owner, slot, me, [strips] + [ring(strips, "blk", k) for k in (1, 2, 3)])
    lo_halo = shifted(halo[1], "slab", 1)
    hi_halo = shifted(halo[0], "slab", -1)
    act, stat = own_layers(live, z0, z1, halo, weight, norm)
    lo_stat = shifted(stat, "slab", 1)
    hi_stat = shifted(stat, "slab", -1)
    return final(live, volume, lo, hi, lo_halo, hi_halo, lo_stat, hi_stat, act, weight, depth)


def solution(mesh):
    return jax.shard_map(
        body,
        mesh=mesh,
        in_specs=(
            P("slab", "blk", None, None, None),
            P("slab", "blk"),
            P(None, "blk", None, None),
            P(None, "blk", None),
            P(),
            P(),
            P(),
            P(),
        ),
        out_specs=P("slab", "blk", None, None, None),
        check_vma=False,
    )
```

```python
import functools
import jax
import jax.numpy as jnp
from jax import lax
from jax.sharding import PartitionSpec as P
import jax.experimental.pallas as pl
import jax.experimental.pallas.tpu as pltpu

LANES = 128
SLOTS = 3
BF = jnp.bfloat16
F32 = jnp.float32
VM = pl.BlockSpec(memory_space=pltpu.VMEM)
SM = pl.BlockSpec(memory_space=pltpu.SMEM)
HB = pl.BlockSpec(memory_space=pltpu.HBM)


def lane_ids(rows):
    return lax.broadcasted_iota(jnp.int32, (rows, LANES), 1)


def roll(x, k):
    return pltpu.roll(x, k % LANES, 1)


def params(mib):
    return pltpu.CompilerParams(vmem_limit_bytes=mib * 2**20)


def split_kernel(side_ref, me_ref, vol_ref, live_ref, near_ref, far_ref, strip_ref, kept_ref, live_s, sems, live_sem):
    c, n = near_ref.shape[1:]
    copies = [pltpu.make_async_copy(vol_ref.at[0, b], kept_ref.at[b], sems.at[b]) for b in range(SLOTS)]
    for copy in copies:
        copy.start()
    lives = pltpu.make_async_copy(live_ref, live_s, live_sem)
    lives.start()
    side = side_ref[0]
    i = lax.broadcasted_iota(jnp.int32, (2 * c, 2 * c), 0)
    j = lax.broadcasted_iota(jnp.int32, (2 * c, 2 * c), 1)
    order = jnp.where(j == jnp.where(i < c, 2 * i + 1 - side, 2 * (i - c) + side), 1.0, 0.0).astype(BF)
    lane = lane_ids(2 * c)
    lives.wait()
    for b in range(SLOTS):
        copies[b].wait()
        x = kept_ref[b].reshape(2 * c, n)
        d = jnp.dot(order, x, preferred_element_type=F32).astype(BF)
        near_ref[b] = d[:c]
        far_ref[b] = d[c:]
        live = jnp.where(live_s[0, b] > 0, 1.0, 0.0).astype(BF)
        rows = jnp.where(lane < 64, d[:, :LANES], d[:, n - LANES:])
        cols = jnp.zeros((2 * c, LANES), BF)
        for t in range(n // LANES):
            tile = d[:, t * LANES:(t + 1) * LANES]
            cols = jnp.where(lane % 64 == 2 * t, roll(tile, 2 * t - 63), cols)
            cols = jnp.where(lane % 64 == (2 * t + 63) % 64, roll(tile, 2 * t + 63), cols)
        rows = rows * live
        cols = cols * live
        for q in range(2):
            strip_ref[q, b, 0] = rows[q * c:(q + 1) * c]
            strip_ref[q, b, 1] = cols[q * c:(q + 1) * c]


def split(side, me, vol, tissue):
    _, s, c, z, n = vol.shape
    return pl.pallas_call(
        split_kernel, name="split",
        in_specs=[SM, SM, HB, HB], out_specs=[VM] * 4,
        out_shape=[jax.ShapeDtypeStruct((s, c, n), BF)] * 2
        + [jax.ShapeDtypeStruct((2, s, 2, c, LANES), BF),
           jax.ShapeDtypeStruct((s, c, z, n), BF)],
        scratch_shapes=[pltpu.SMEM((1, s), jnp.int32), pltpu.SemaphoreType.DMA((SLOTS,)), pltpu.SemaphoreType.DMA],
        compiler_params=params(24),
    )(side, me, pltpu.with_memory_space_constraint(vol, pltpu.HBM), pltpu.with_memory_space_constraint(tissue, pltpu.HBM))


def conv_layer(x_at, rows, cols, weight, stack, emit):
    c = rows.shape[0]
    tiles = stack.shape[1] // LANES - 1
    lane = lane_ids(c)
    first = lane % 64 == 0
    last = lane % 64 == 63
    low = lane < 64
    for t in range(tiles + 1):
        at = slice(t * LANES, (t + 1) * LANES)
        tile = x_at(t) if t < tiles else rows
        edge = roll(cols, -2 * t) if t < tiles else jnp.zeros((c, LANES), BF)
        stack[0:c, at] = jnp.where(first, edge, roll(tile, 1))
        stack[c:2 * c, at] = tile
        stack[2 * c:, at] = jnp.where(last, edge, roll(tile, -1))

    def mix(start, size):
        return jnp.dot(weight, stack[:, start:start + size], preferred_element_type=F32)

    outer = mix(tiles * LANES, LANES)
    above, end = outer[:c], outer[2 * c:]
    middle = turned = None
    for pair in range(tiles // 2):
        u = mix(pair * 2 * LANES, 2 * LANES)
        for h in range(2):
            part = u[:, h * LANES:(h + 1) * LANES]
            turn = roll(above + part[2 * c:], 64)
            t = 2 * pair + h
            if t:
                emit(t - 1, middle + jnp.where(low, turned, turn))
            above, middle, turned = part[:c], part[c:2 * c], turn
    turn = roll(above + end, 64)
    emit(tiles - 1, middle + jnp.where(low, turned, turn))


def tap_rows(weight):
    width = weight.shape[1] // 3
    return jnp.concatenate([weight[:, a * width:(a + 1) * width] for a in range(3)], axis=0)


def column(row):
    c = row.shape[1]
    i = lax.broadcasted_iota(jnp.int32, (c, c), 0)
    j = lax.broadcasted_iota(jnp.int32, (c, c), 1)
    return jnp.sum(jnp.where(i == j, jnp.broadcast_to(row, (c, c)), 0.0), axis=1, keepdims=True)


def own_kernel(me_ref, live_ref, owner_ref, slot_ref, weight_ref, gain_ref, bias_ref, near_ref, far_ref,
               own_ref, one_ref, two_ref, three_ref, near_act, far_act, note_ref, table, plane, stack):
    c, n = near_ref.shape[1:]
    lane = lane_ids(c)
    me = me_ref[0]
    for k, ref in enumerate((own_ref, one_ref, two_ref, three_ref)):
        table[k] = ref[...]
    weight = tap_rows(weight_ref[...])
    gain_col = column(gain_ref[...])
    bias_col = column(bias_ref[...])
    scale = 1.0 / (2 * n)
    note = jnp.zeros((c, LANES), F32)

    def pick(t, b, e):
        return lax.rem(me - owner_ref[t, e, 0, b] + 4, 4), slot_ref[t, e, b]

    for b in range(SLOTS):
        south, north, west, east = pick(0, b, 1), pick(0, b, 0), pick(1, b, 0), pick(1, b, 1)
        total = [jnp.zeros((c, LANES), F32)]
        for q, ref in enumerate((near_ref, far_ref)):
            rows = jnp.where(lane < 64, table[south[0], q, south[1], 0], table[north[0], q, north[1], 0])
            cols = jnp.where(lane % 2 == 0, table[west[0], q, west[1], 1], table[east[0], q, east[1], 1])
            if q == 1:
                note_ref[2 * b] = rows
                note_ref[2 * b + 1] = cols

            def emit(t, value, q=q):
                plane[q, :, t * LANES:(t + 1) * LANES] = value
                total[0] += value
            conv_layer(lambda t: ref[b, :, t * LANES:(t + 1) * LANES], rows, cols, weight, stack, emit)
        mean = jnp.sum(total[0], axis=1, keepdims=True) * scale
        mean_b = jnp.broadcast_to(mean, (c, LANES))
        square = jnp.zeros((c, LANES), F32)
        for q in range(2):
            for t in range(n // LANES):
                dev = plane[q, :, t * LANES:(t + 1) * LANES] - mean_b
                square += dev * dev
        var = jnp.sum(square, axis=1, keepdims=True) * scale
        live = jnp.where(live_ref[0, b] > 0, 1.0, 0.0)
        gain_b = jnp.broadcast_to(lax.rsqrt(var + 1e-05) * gain_col * live, (c, LANES))
        bias_b = jnp.broadcast_to(bias_col * live, (c, LANES))
        for q, out in enumerate((near_act, far_act)):
            for t in range(n // LANES):
                at = slice(t * LANES, (t + 1) * LANES)
                out[b, :, at] = jnp.maximum((plane[q, :, at] - mean_b) * gain_b + bias_b, 0.0).astype(BF)
        for k, value in enumerate((mean_b, gain_b, bias_b)):
            note = jnp.where(lane == 3 * b + k, value, note)
    for k in range(3):
        part = note.astype(BF)
        note_ref[2 * SLOTS + k] = part
        note = note - part.astype(F32)


def own_layers(me, live, owner, slot, weight, gain, bias, near, far, strips):
    s, c, n = near.shape
    return pl.pallas_call(
        own_kernel, name="own",
        in_specs=[SM] * 4 + [VM] * 9, out_specs=[VM] * 3,
        out_shape=[jax.ShapeDtypeStruct((s, c, n), BF)] * 2 + [jax.ShapeDtypeStruct((2 * s + 3, c, LANES), BF)],
        scratch_shapes=[pltpu.VMEM((4,) + strips[0].shape, BF), pltpu.VMEM((2, c, n), F32),
                        pltpu.VMEM((3 * c, n + LANES), BF)],
        compiler_params=params(16),
    )(me, live, owner, slot, weight, gain, bias, near, far, *strips)


def final_kernel(side_ref, live_ref, weight_ref, depth_ref, kept_ref, raw_ref, note_ref, near_in_ref, near_ref, far_ref,
                 out_ref, stack, taps, done, sems):
    c, n = near_ref.shape[1:]
    side = side_ref[0]
    weight = tap_rows(weight_ref[...])
    k = lax.broadcasted_iota(jnp.int32, (3 * c, 4 * c), 0)
    j = lax.broadcasted_iota(jnp.int32, (3 * c, 4 * c), 1)
    oi = lax.broadcasted_iota(jnp.int32, (2 * c, c), 0)
    oj = lax.broadcasted_iota(jnp.int32, (2 * c, c), 1)
    depth = jnp.zeros((2 * c, 4 * c), F32)
    for z in range(2):
        layer = k // c + z
        place = jnp.where(side > 0, layer, 3 - layer) * c + k % c
        spread = jnp.where(j == place, 1.0, 0.0).astype(BF)
        part = jnp.dot(depth_ref[...], spread, preferred_element_type=F32).astype(BF)
        pick = jnp.where(oi == 2 * oj + z, 1.0, 0.0).astype(BF)
        depth += jnp.dot(pick, part, preferred_element_type=F32)
    depth = depth.astype(BF)
    stats = note_ref[2 * SLOTS].astype(F32) + note_ref[2 * SLOTS + 1].astype(F32) + note_ref[2 * SLOTS + 2].astype(F32)
    wide = 512
    copies = []
    for b in range(SLOTS):
        mean, gain, bias = (jnp.broadcast_to(stats[:, 3 * b + i:3 * b + i + 1], (c, LANES)) for i in range(3))

        def emit(t, value):
            stack[3 * c:, t * LANES:(t + 1) * LANES] = jnp.maximum((value - mean) * gain + bias, 0.0).astype(BF)
        conv_layer(lambda t: raw_ref[b, :, t * LANES:(t + 1) * LANES], note_ref[2 * b], note_ref[2 * b + 1],
                   weight, taps, emit)
        stack[0:c] = near_in_ref[b]
        stack[c:2 * c] = near_ref[b]
        stack[2 * c:3 * c] = far_ref[b]
        live = jnp.where(live_ref[0, b] > 0, 1.0, 0.0)
        for w in range(n // wide):
            at = slice(w * wide, (w + 1) * wide)
            mixed = jnp.dot(depth, stack[:, at], preferred_element_type=F32)
            given = kept_ref[b, :, :, at].reshape(2 * c, wide).astype(F32)
            done[b, :, :, at] = ((given + mixed) * live).astype(BF).reshape(c, 2, wide)
        copies.append(pltpu.make_async_copy(done.at[b], out_ref.at[0, b], sems.at[b]))
        copies[-1].start()
    for copy in copies:
        copy.wait()


def final(side, live, weight, depth, kept, raw, note, near_in, near, far):
    s, c, z, n = kept.shape
    return pl.pallas_call(
        final_kernel, name="final",
        in_specs=[SM] * 2 + [VM] * 8, out_specs=HB,
        out_shape=jax.ShapeDtypeStruct((1, s, c, z, n), BF),
        scratch_shapes=[pltpu.VMEM((4 * c, n), BF), pltpu.VMEM((3 * c, n + LANES), BF), pltpu.VMEM((s, c, z, n), BF),
                        pltpu.SemaphoreType.DMA((SLOTS,))],
        compiler_params=params(16),
    )(side, live, weight, depth, kept, raw, note, near_in, near, far)


def swap(value, axis, first):
    count = lax.axis_size(axis)
    pairs = []
    for i in range(first, count - 1, 2):
        pairs += [(i, i + 1), (i + 1, i)]
    return lax.ppermute(value, axis, pairs)


def ring(value, axis, steps):
    count = lax.axis_size(axis)
    return lax.ppermute(value, axis, [(i, (i + steps) % count) for i in range(count)])


def body(volume, tissue, face_owner, face_slot, plane_weight, depth_weight, norm_gain, norm_bias):
    owner = jnp.transpose(face_owner, (0, 2, 3, 1))
    slot = jnp.transpose(face_slot, (0, 2, 1))
    gain = norm_gain.reshape(1, -1)
    bias = norm_bias.reshape(1, -1)
    me = lax.axis_index("blk").reshape(1)
    side = (lax.axis_index("slab") % 2).reshape(1)
    near, far, strips, kept = split(side, me, volume, tissue)
    raw = swap(far, "slab", 1)
    strips = [strips] + [ring(strips, "blk", k) for k in (1, 2, 3)]
    near_act, far_act, note = own_layers(me, tissue, owner, slot, plane_weight, gain, bias, near, far, strips)
    note_in = swap(note, "slab", 1)
    near_in = swap(near_act, "slab", 0)
    return final(side, tissue, plane_weight, depth_weight, kept, raw, note_in, near_in, near_act, far_act)


def solution(mesh):
    return jax.shard_map(
        body,
        mesh=mesh,
        in_specs=(
            P("slab", "blk", None, None, None),
            P("slab", "blk"),
            P(None, "blk", None, None),
            P(None, "blk", None),
            P(),
            P(),
            P(),
            P(),
        ),
        out_specs=P("slab", "blk", None, None, None),
        check_vma=False,
    )
```

```python
import functools
import jax
import jax.numpy as jnp
from jax import lax
from jax.sharding import PartitionSpec as P
import jax.experimental.pallas as pl
import jax.experimental.pallas.tpu as pltpu

LANES = 128
SLOTS = 3
BF = jnp.bfloat16
F32 = jnp.float32
VM = pl.BlockSpec(memory_space=pltpu.VMEM)
SM = pl.BlockSpec(memory_space=pltpu.SMEM)
HB = pl.BlockSpec(memory_space=pltpu.HBM)


def lane_ids(rows):
    return lax.broadcasted_iota(jnp.int32, (rows, LANES), 1)


def roll(x, k):
    return pltpu.roll(x, k % LANES, 1)


def params(mib):
    return pltpu.CompilerParams(vmem_limit_bytes=mib * 2**20)


def cost(us):
    return pl.CostEstimate(flops=us * 1_000_000_000, bytes_accessed=us * 1_000_000, transcendentals=0)


def split_kernel(side_ref, me_ref, vol_ref, live_ref, near_ref, far_ref, strip_ref, kept_ref, live_s, sems, live_sem):
    c, n = near_ref.shape[1:]
    copies = [pltpu.make_async_copy(vol_ref.at[0, b], kept_ref.at[b], sems.at[b]) for b in range(SLOTS)]
    for copy in copies:
        copy.start()
    lives = pltpu.make_async_copy(live_ref, live_s, live_sem)
    lives.start()
    side = side_ref[0]
    i = lax.broadcasted_iota(jnp.int32, (2 * c, 2 * c), 0)
    j = lax.broadcasted_iota(jnp.int32, (2 * c, 2 * c), 1)
    order = jnp.where(j == jnp.where(i < c, 2 * i + 1 - side, 2 * (i - c) + side), 1.0, 0.0).astype(BF)
    lane = lane_ids(2 * c)
    lives.wait()
    for b in range(SLOTS):
        copies[b].wait()
        x = kept_ref[b].reshape(2 * c, n)
        d = jnp.dot(order, x, preferred_element_type=F32).astype(BF)
        near_ref[b] = d[:c]
        far_ref[b] = d[c:]
        live = jnp.where(live_s[0, b] > 0, 1.0, 0.0).astype(BF)
        rows = jnp.where(lane < 64, d[:, :LANES], d[:, n - LANES:])
        cols = jnp.zeros((2 * c, LANES), BF)
        for t in range(n // LANES):
            tile = d[:, t * LANES:(t + 1) * LANES]
            cols = jnp.where(lane % 64 // 2 == t, roll(tile, 2 * t + 65), cols)
        rows = rows * live
        cols = cols * live
        for q in range(2):
            strip_ref[q, b, 0] = rows[q * c:(q + 1) * c]
            strip_ref[q, b, 1] = cols[q * c:(q + 1) * c]


def split(side, me, vol, tissue):
    _, s, c, z, n = vol.shape
    return pl.pallas_call(
        split_kernel, name="split",
        in_specs=[SM, SM, HB, HB], out_specs=[VM] * 4,
        out_shape=[jax.ShapeDtypeStruct((s, c, n), BF)] * 2
        + [jax.ShapeDtypeStruct((2, s, 2, c, LANES), BF),
           jax.ShapeDtypeStruct((s, c, z, n), BF)],
        scratch_shapes=[pltpu.SMEM((1, s), jnp.int32), pltpu.SemaphoreType.DMA((SLOTS,)), pltpu.SemaphoreType.DMA],
        compiler_params=params(24),
    )(side, me, pltpu.with_memory_space_constraint(vol, pltpu.HBM), pltpu.with_memory_space_constraint(tissue, pltpu.HBM))


def conv_layer(x_at, weight, stack, emit):
    c, n = weight.shape[0] // 3, stack.shape[1]
    tiles = n // LANES
    lane = lane_ids(c)
    zero = jnp.zeros((c, LANES), BF)
    low = lane < 64
    for t in range(tiles):
        at = slice(t * LANES, (t + 1) * LANES)
        tile = x_at(t)
        stack[0:c, at] = jnp.where(lane % 64 == 0, zero, roll(tile, 1))
        stack[c:2 * c, at] = tile
        stack[2 * c:, at] = jnp.where(lane % 64 == 63, zero, roll(tile, -1))
    above = jnp.zeros((c, LANES), F32)
    middle = turned = None
    for pair in range(tiles // 2):
        u = jnp.dot(weight, stack[:, pair * 2 * LANES:(pair + 1) * 2 * LANES], preferred_element_type=F32)
        for h in range(2):
            part = u[:, h * LANES:(h + 1) * LANES]
            turn = roll(above + part[2 * c:], 64)
            t = 2 * pair + h
            if t:
                emit(t - 1, middle + jnp.where(low, turned, turn))
            above, middle, turned = part[:c], part[c:2 * c], turn
    emit(tiles - 1, middle + jnp.where(low, turned, roll(above, 64)))


def edge_terms(rows, cols, weight):
    c = rows.shape[0]
    lane = lane_ids(c)
    zero = jnp.zeros((c, LANES), BF)
    low = lane < 64
    even = lane % 2 == 0
    row_taps = jnp.concatenate([jnp.where(lane % 64 == 0, zero, roll(rows, 1)), rows,
                                jnp.where(lane % 64 == 63, zero, roll(rows, -1))], axis=0)
    col_taps = jnp.concatenate([jnp.where(even, cols, zero), zero, jnp.where(even, zero, cols)], axis=0)
    u = jnp.dot(weight, jnp.concatenate([row_taps, col_taps], axis=1), preferred_element_type=F32)
    top = jnp.where(low, roll(u[:c, :LANES], 64), 0.0)
    bottom = jnp.where(low, 0.0, roll(u[2 * c:, :LANES], 64))
    v = u[:, LANES:]
    place = jnp.where(even, lane, (lane + 65) % LANES)
    upper = jnp.where(place < 64, jnp.where(place == 0, 0.0, roll(v[:c], 66)), roll(v[:c], 64))
    lower = jnp.where(place < 64, roll(v[2 * c:], 64), jnp.where(place == 126, 0.0, roll(v[2 * c:], 62)))
    return top, bottom, v[c:2 * c] + upper + lower


def with_edges(value, t, tiles, terms):
    top, bottom, strip = terms
    lane = lane_ids(value.shape[0])
    value = value + jnp.where((lane + 1) % 64 < 2, roll(strip, -2 * t), 0.0)
    if t == 0:
        value = value + top
    if t == tiles - 1:
        value = value + bottom
    return value


def tap_rows(weight):
    width = weight.shape[1] // 3
    return jnp.concatenate([weight[:, a * width:(a + 1) * width] for a in range(3)], axis=0)


def column(row):
    c = row.shape[1]
    i = lax.broadcasted_iota(jnp.int32, (c, c), 0)
    j = lax.broadcasted_iota(jnp.int32, (c, c), 1)
    return jnp.sum(jnp.where(i == j, jnp.broadcast_to(row, (c, c)), 0.0), axis=1, keepdims=True)


def bulk_kernel(weight_ref, near_ref, far_ref, plane_ref, sum_ref, stack):
    c, n = near_ref.shape[1:]
    weight = tap_rows(weight_ref[...])
    for b in range(SLOTS):
        total = [jnp.zeros((c, LANES), F32)]
        for q, ref in enumerate((near_ref, far_ref)):
            def emit(t, value):
                plane_ref[q, b, :, t * LANES:(t + 1) * LANES] = value
                total[0] += value
            conv_layer(lambda t: ref[b, :, t * LANES:(t + 1) * LANES], weight, stack, emit)
        sum_ref[b] = total[0]


def bulk(weight, near, far):
    s, c, n = near.shape
    return pl.pallas_call(
        bulk_kernel, name="bulk",
        in_specs=[VM] * 3, out_specs=[VM] * 2,
        out_shape=[jax.ShapeDtypeStruct((2, s, c, n), F32), jax.ShapeDtypeStruct((s, c, LANES), F32)],
        scratch_shapes=[pltpu.VMEM((3 * c, n), BF)],
        compiler_params=params(8), cost_estimate=cost(5),
    )(weight, near, far)


def own_kernel(me_ref, live_ref, owner_ref, slot_ref, weight_ref, gain_ref, bias_ref, plane_ref, sum_ref,
               own_ref, one_ref, two_ref, three_ref, near_act, far_act, note_ref, table, off, edge):
    c, n = near_act.shape[1:]
    tiles = n // LANES
    lane = lane_ids(c)
    me = me_ref[0]
    for k, ref in enumerate((own_ref, one_ref, two_ref, three_ref)):
        table[k] = ref[...]
    weight = tap_rows(weight_ref[...])
    gain_col = column(gain_ref[...])
    bias_col = column(bias_ref[...])
    scale = 1.0 / (2 * n)
    note = jnp.zeros((c, LANES), F32)

    def pick(t, b, e):
        return lax.rem(me - owner_ref[t, e, 0, b] + 4, 4), slot_ref[t, e, b]

    means, squares = [], []
    for b in range(SLOTS):
        south, north, west, east = pick(0, b, 1), pick(0, b, 0), pick(1, b, 0), pick(1, b, 1)
        total = sum_ref[b]
        terms = []
        for q in range(2):
            rows = jnp.where(lane < 64, table[south[0], q, south[1], 0], table[north[0], q, north[1], 0])
            cols = jnp.where(lane % 2 == 0, table[west[0], q, west[1], 1],
                             roll(table[east[0], q, east[1], 1], -2))
            if q == 1:
                note_ref[2 * b] = rows
                note_ref[2 * b + 1] = cols
            for k, term in enumerate(edge_terms(rows, cols, weight)):
                edge[b, q, k] = term
                total += term
        means.append(jnp.broadcast_to(jnp.sum(total, axis=1, keepdims=True) * scale, (c, LANES)))
    for b in range(SLOTS):
        square = jnp.zeros((c, LANES), F32)
        for q in range(2):
            terms = [edge[b, q, k] for k in range(3)]
            for t in range(tiles):
                at = slice(t * LANES, (t + 1) * LANES)
                value = with_edges(plane_ref[q, b, :, at], t, tiles, terms) - means[b]
                off[b, q, :, at] = value
                square += value * value
        squares.append(square)
    for b in range(SLOTS):
        var = jnp.sum(squares[b], axis=1, keepdims=True) * scale
        live = jnp.where(live_ref[0, b] > 0, 1.0, 0.0)
        gain_b = jnp.broadcast_to(lax.rsqrt(var + 1e-05) * gain_col * live, (c, LANES))
        bias_b = jnp.broadcast_to(bias_col * live, (c, LANES))
        for q, out in enumerate((near_act, far_act)):
            for t in range(tiles):
                at = slice(t * LANES, (t + 1) * LANES)
                out[b, :, at] = jnp.maximum(off[b, q, :, at] * gain_b + bias_b, 0.0).astype(BF)
        for k, value in enumerate((means[b], gain_b, bias_b)):
            note = jnp.where(lane == 3 * b + k, value, note)
    for k in range(3):
        part = note.astype(BF)
        note_ref[2 * SLOTS + k] = part
        note = note - part.astype(F32)


def own_layers(me, live, owner, slot, weight, gain, bias, plane, sums, strips):
    _, s, c, n = plane.shape
    return pl.pallas_call(
        own_kernel, name="own",
        in_specs=[SM] * 4 + [VM] * 9, out_specs=[VM] * 3,
        out_shape=[jax.ShapeDtypeStruct((s, c, n), BF)] * 2 + [jax.ShapeDtypeStruct((2 * s + 3, c, LANES), BF)],
        scratch_shapes=[pltpu.VMEM((4,) + strips[0].shape, BF), pltpu.VMEM((s, 2, c, n), F32),
                        pltpu.VMEM((s, 2, 3, c, LANES), F32)],
        compiler_params=params(12), cost_estimate=cost(0),
    )(me, live, owner, slot, weight, gain, bias, plane, sums, *strips)


def depth_matrix(side, depth):
    c = depth.shape[0]
    k = lax.broadcasted_iota(jnp.int32, (3 * c, 4 * c), 0)
    j = lax.broadcasted_iota(jnp.int32, (3 * c, 4 * c), 1)
    oi = lax.broadcasted_iota(jnp.int32, (2 * c, c), 0)
    oj = lax.broadcasted_iota(jnp.int32, (2 * c, c), 1)
    total = jnp.zeros((2 * c, 4 * c), F32)
    for z in range(2):
        layer = k // c + z
        place = jnp.where(side > 0, layer, 3 - layer) * c + k % c
        spread = jnp.where(j == place, 1.0, 0.0).astype(BF)
        part = jnp.dot(depth, spread, preferred_element_type=F32).astype(BF)
        pick = jnp.where(oi == 2 * oj + z, 1.0, 0.0).astype(BF)
        total += jnp.dot(pick, part, preferred_element_type=F32)
    return total.astype(BF)


def inner_kernel(side_ref, weight_ref, depth_ref, kept_ref, raw_ref, near_ref, far_ref, plane_ref, part_ref, matrix_ref,
                 stack, taps):
    c, n = near_ref.shape[1:]
    weight = tap_rows(weight_ref[...])
    depth = depth_matrix(side_ref[0], depth_ref[...])
    matrix_ref[...] = jnp.concatenate([depth[:, :c], depth[:, 3 * c:]], axis=1)
    mine = depth[:, c:3 * c]
    wide = 512
    for b in range(SLOTS):
        stack[0:c] = near_ref[b]
        stack[c:] = far_ref[b]
        for w in range(n // wide):
            at = slice(w * wide, (w + 1) * wide)
            part_ref[b, :, at] = (jnp.dot(mine, stack[:, at], preferred_element_type=F32)
                                  + kept_ref[b, :, :, at].reshape(2 * c, wide).astype(F32))

        def emit(t, value):
            plane_ref[b, :, t * LANES:(t + 1) * LANES] = value
        conv_layer(lambda t: raw_ref[b, :, t * LANES:(t + 1) * LANES], weight, taps, emit)


def inner(side, weight, depth, kept, raw, near, far):
    s, c, n = near.shape
    return pl.pallas_call(
        inner_kernel, name="inner",
        in_specs=[SM] + [VM] * 6, out_specs=[VM] * 3,
        out_shape=[jax.ShapeDtypeStruct((s, c, n), F32), jax.ShapeDtypeStruct((s, 2 * c, n), F32),
                   jax.ShapeDtypeStruct((2 * c, 2 * c), BF)],
        scratch_shapes=[pltpu.VMEM((2 * c, n), BF), pltpu.VMEM((3 * c, n), BF)],
        compiler_params=params(8), cost_estimate=cost(100),
    )(side, weight, depth, kept, raw, near, far)


def final_kernel(live_ref, weight_ref, matrix_ref, plane_ref, part_ref, note_ref, near_in_ref, out_ref, stack, done, edge, norm, sems):
    c, n = near_in_ref.shape[1:]
    tiles = n // LANES
    weight = tap_rows(weight_ref[...])
    matrix = matrix_ref[...]
    stats = note_ref[2 * SLOTS].astype(F32) + note_ref[2 * SLOTS + 1].astype(F32) + note_ref[2 * SLOTS + 2].astype(F32)
    wide = 512
    copies = []
    for b in range(SLOTS):
        for k, term in enumerate(edge_terms(note_ref[2 * b], note_ref[2 * b + 1], weight)):
            edge[b, k] = term
        for k in range(3):
            norm[b, k] = jnp.broadcast_to(stats[:, 3 * b + k:3 * b + k + 1], (c, LANES))
    for b in range(SLOTS):
        mean, gain, bias = (norm[b, k] for k in range(3))
        terms = [edge[b, k] for k in range(3)]
        stack[0:c] = near_in_ref[b]
        for t in range(tiles):
            at = slice(t * LANES, (t + 1) * LANES)
            value = with_edges(plane_ref[b, :, at], t, tiles, terms) - mean
            stack[c:, at] = jnp.maximum(value * gain + bias, 0.0).astype(BF)
        live = jnp.where(live_ref[0, b] > 0, 1.0, 0.0)
        for w in range(n // wide):
            at = slice(w * wide, (w + 1) * wide)
            mixed = jnp.dot(matrix, stack[:, at], preferred_element_type=F32)
            done[b, :, :, at] = ((part_ref[b, :, at] + mixed) * live).astype(BF).reshape(c, 2, wide)
        copies.append(pltpu.make_async_copy(done.at[b], out_ref.at[0, b], sems.at[b]))
        copies[-1].start()
    for copy in copies:
        copy.wait()


def final(live, weight, matrix, plane, part, note, near_in):
    s, c, n = near_in.shape
    return pl.pallas_call(
        final_kernel, name="final",
        in_specs=[SM] + [VM] * 6, out_specs=HB,
        out_shape=jax.ShapeDtypeStruct((1, s, c, 2, n), BF),
        scratch_shapes=[pltpu.VMEM((2 * c, n), BF), pltpu.VMEM((s, c, 2, n), BF),
                        pltpu.VMEM((s, 3, c, LANES), F32), pltpu.VMEM((s, 3, c, LANES), F32), pltpu.SemaphoreType.DMA((SLOTS,))],
        compiler_params=params(12), cost_estimate=cost(2),
    )(live, weight, matrix, plane, part, note, near_in)


def swap(value, axis, first):
    count = lax.axis_size(axis)
    pairs = []
    for i in range(first, count - 1, 2):
        pairs += [(i, i + 1), (i + 1, i)]
    return lax.ppermute(value, axis, pairs)


def ring(value, axis, steps):
    count = lax.axis_size(axis)
    return lax.ppermute(value, axis, [(i, (i + steps) % count) for i in range(count)])


def body(volume, tissue, face_owner, face_slot, plane_weight, depth_weight, norm_gain, norm_bias):
    owner = jnp.transpose(face_owner, (0, 2, 3, 1))
    slot = jnp.transpose(face_slot, (0, 2, 1))
    gain = norm_gain.reshape(1, -1)
    bias = norm_bias.reshape(1, -1)
    me = lax.axis_index("blk").reshape(1)
    side = (lax.axis_index("slab") % 2).reshape(1)
    near, far, strips, kept = split(side, me, volume, tissue)
    raw = swap(far, "slab", 1)
    strips = [strips] + [ring(strips, "blk", k) for k in (1, 2, 3)]
    plane, sums = bulk(plane_weight, near, far)
    near_act, far_act, note = own_layers(me, tissue, owner, slot, plane_weight, gain, bias, plane, sums, strips)
    note_in = swap(note, "slab", 1)
    near_in = swap(near_act, "slab", 0)
    far_plane, part, matrix = inner(side, plane_weight, depth_weight, kept, raw, near_act, far_act)
    return final(tissue, plane_weight, matrix, far_plane, part, note_in, near_in)


def solution(mesh):
    return jax.shard_map(
        body,
        mesh=mesh,
        in_specs=(
            P("slab", "blk", None, None, None),
            P("slab", "blk"),
            P(None, "blk", None, None),
            P(None, "blk", None),
            P(),
            P(),
            P(),
            P(),
        ),
        out_specs=P("slab", "blk", None, None, None),
        check_vma=False,
    )
```

```python
import functools
import jax
import jax.numpy as jnp
from jax import lax
from jax.sharding import PartitionSpec as P
import jax.experimental.pallas as pl
import jax.experimental.pallas.tpu as pltpu

LANES = 128
SLOTS = 3
BF = jnp.bfloat16
F32 = jnp.float32
VM = pl.BlockSpec(memory_space=pltpu.VMEM)
SM = pl.BlockSpec(memory_space=pltpu.SMEM)
HB = pl.BlockSpec(memory_space=pltpu.HBM)


def lane_ids(rows):
    return lax.broadcasted_iota(jnp.int32, (rows, LANES), 1)


def roll(x, k):
    return pltpu.roll(x, k % LANES, 1)


def params(mib):
    return pltpu.CompilerParams(vmem_limit_bytes=mib * 2**20)


def cost(us):
    return pl.CostEstimate(flops=us * 1_000_000_000, bytes_accessed=us * 1_000_000, transcendentals=0)


def split_kernel(side_ref, me_ref, vol_ref, live_ref, near_ref, far_ref, strip_ref, kept_ref, live_s, sems, live_sem):
    c, n = near_ref.shape[1:]
    copies = [pltpu.make_async_copy(vol_ref.at[0, b], kept_ref.at[b], sems.at[b]) for b in range(SLOTS)]
    for copy in copies:
        copy.start()
    lives = pltpu.make_async_copy(live_ref, live_s, live_sem)
    lives.start()
    side = side_ref[0]
    i = lax.broadcasted_iota(jnp.int32, (2 * c, 2 * c), 0)
    j = lax.broadcasted_iota(jnp.int32, (2 * c, 2 * c), 1)
    order = jnp.where(j == jnp.where(i < c, 2 * i + 1 - side, 2 * (i - c) + side), 1.0, 0.0).astype(BF)
    lane = lane_ids(2 * c)
    edge = (lane + 1) % 64 < 2
    zero = jnp.zeros((2 * c, LANES), BF)
    lives.wait()
    for b in range(SLOTS):
        copies[b].wait()
        x = kept_ref[b].reshape(2 * c, n)
        d = jnp.dot(order, x, preferred_element_type=F32).astype(BF)
        near_ref[b] = d[:c]
        far_ref[b] = d[c:]
        live = jnp.where(live_s[0, b] > 0, 1.0, 0.0).astype(BF)
        rows = jnp.where(lane < 64, d[:, :LANES], d[:, n - LANES:])
        cols = zero
        for t in range(n // LANES):
            tile = jnp.where(edge, d[:, t * LANES:(t + 1) * LANES], zero)
            cols += roll(tile, 2 * t + 65)
        rows = rows * live
        cols = cols * live
        for q in range(2):
            strip_ref[q, b, 0] = rows[q * c:(q + 1) * c]
            strip_ref[q, b, 1] = cols[q * c:(q + 1) * c]


def split(side, me, vol, tissue):
    _, s, c, z, n = vol.shape
    return pl.pallas_call(
        split_kernel, name="split",
        in_specs=[SM, SM, HB, HB], out_specs=[VM] * 4,
        out_shape=[jax.ShapeDtypeStruct((s, c, n), BF)] * 2
        + [jax.ShapeDtypeStruct((2, s, 2, c, LANES), BF),
           jax.ShapeDtypeStruct((s, c, z, n), BF)],
        scratch_shapes=[pltpu.SMEM((1, s), jnp.int32), pltpu.SemaphoreType.DMA((SLOTS,)), pltpu.SemaphoreType.DMA],
        compiler_params=params(24),
    )(side, me, pltpu.with_memory_space_constraint(vol, pltpu.HBM), pltpu.with_memory_space_constraint(tissue, pltpu.HBM))


def conv_layer(x_at, weight, stack, emit):
    c, n = stack.shape[1:]
    tiles = n // LANES
    lane = lane_ids(c)
    zero = jnp.zeros((c, LANES), BF)
    low = lane < 64
    for t in range(tiles):
        at = slice(t * LANES, (t + 1) * LANES)
        tile = x_at(at)
        stack[0, :, at] = jnp.where(lane % 64 == 0, zero, roll(tile, 1))
        stack[1, :, at] = jnp.where(lane % 64 == 63, zero, roll(tile, -1))
    above = jnp.zeros((c, LANES), F32)
    middle = turned = None
    for pair in range(tiles // 2):
        at = slice(pair * 2 * LANES, (pair + 1) * 2 * LANES)
        taps = jnp.concatenate([stack[0, :, at], x_at(at), stack[1, :, at]], axis=0)
        u = jnp.dot(weight, taps, preferred_element_type=F32)
        for h in range(2):
            part = u[:, h * LANES:(h + 1) * LANES]
            turn = roll(above + part[2 * c:], 64)
            t = 2 * pair + h
            if t:
                emit(t - 1, middle + jnp.where(low, turned, turn))
            above, middle, turned = part[:c], part[c:2 * c], turn
    emit(tiles - 1, middle + jnp.where(low, turned, roll(above, 64)))


def edge_terms(rows, cols, weight):
    c = rows.shape[0]
    lane = lane_ids(c)
    zero = jnp.zeros((c, LANES), BF)
    low = lane < 64
    even = lane % 2 == 0
    row_taps = jnp.concatenate([jnp.where(lane % 64 == 0, zero, roll(rows, 1)), rows,
                                jnp.where(lane % 64 == 63, zero, roll(rows, -1))], axis=0)
    col_taps = jnp.concatenate([jnp.where(even, cols, zero), zero, jnp.where(even, zero, cols)], axis=0)
    u = jnp.dot(weight, jnp.concatenate([row_taps, col_taps], axis=1), preferred_element_type=F32)
    top = jnp.where(low, roll(u[:c, :LANES], 64), 0.0)
    bottom = jnp.where(low, 0.0, roll(u[2 * c:, :LANES], 64))
    v = u[:, LANES:]
    place = jnp.where(even, lane, (lane + 65) % LANES)
    upper = jnp.where(place < 64, jnp.where(place == 0, 0.0, roll(v[:c], 66)), roll(v[:c], 64))
    lower = jnp.where(place < 64, roll(v[2 * c:], 64), jnp.where(place == 126, 0.0, roll(v[2 * c:], 62)))
    return top, bottom, v[c:2 * c] + upper + lower


def with_edges(value, t, tiles, terms):
    top, bottom, strip = terms
    lane = lane_ids(value.shape[0])
    value = value + jnp.where((lane + 1) % 64 < 2, roll(strip, -2 * t), 0.0)
    if t == 0:
        value = value + top
    if t == tiles - 1:
        value = value + bottom
    return value


def tap_rows(weight):
    width = weight.shape[1] // 3
    return jnp.concatenate([weight[:, a * width:(a + 1) * width] for a in range(3)], axis=0)


def column(row):
    c = row.shape[1]
    i = lax.broadcasted_iota(jnp.int32, (c, c), 0)
    j = lax.broadcasted_iota(jnp.int32, (c, c), 1)
    return jnp.sum(jnp.where(i == j, jnp.broadcast_to(row, (c, c)), 0.0), axis=1, keepdims=True)


def bulk_kernel(weight_ref, near_ref, far_ref, plane_ref, found_ref, stack):
    c, n = near_ref.shape[1:]
    tiles = n // LANES
    weight = tap_rows(weight_ref[...])
    lane = lane_ids(c)
    edge = (lane + 1) % 64 < 2
    low = lane < 64
    inside = 2 * (n - 4 * 64 + 4)
    for b in range(SLOTS):
        total = [jnp.zeros((c, LANES), F32)]
        outer = jnp.zeros((c, LANES), F32)
        for q, ref in enumerate((near_ref, far_ref)):
            def emit(t, value):
                plane_ref[q, b, :, t * LANES:(t + 1) * LANES] = value
                total[0] += value
            conv_layer(lambda at: ref[b, :, at], weight, stack, emit)
            strip = jnp.zeros((c, LANES), F32)
            for t in range(tiles):
                strip += roll(jnp.where(edge, plane_ref[q, b, :, t * LANES:(t + 1) * LANES], 0.0), 2 * t)
            rows = jnp.where(low, plane_ref[q, b, :, :LANES], plane_ref[q, b, :, n - LANES:])
            rows = jnp.where(edge, 0.0, rows)
            found_ref[b, 2 + q] = strip
            found_ref[b, 4 + q] = rows
            outer += strip + rows
        mean = jnp.sum(total[0] - outer, axis=1, keepdims=True) * (1.0 / inside)
        mean = jnp.broadcast_to(mean, (c, LANES))
        square = jnp.zeros((c, LANES), F32)
        for q in range(2):
            for t in range(tiles):
                off = jnp.where(edge, 0.0, plane_ref[q, b, :, t * LANES:(t + 1) * LANES] - mean)
                if t == 0:
                    off = jnp.where(low, 0.0, off)
                if t == tiles - 1:
                    off = jnp.where(low, off, 0.0)
                square += off * off
        found_ref[b, 0] = square
        found_ref[b, 1] = mean


def bulk(weight, near, far):
    s, c, n = near.shape
    return pl.pallas_call(
        bulk_kernel, name="bulk",
        in_specs=[VM] * 3, out_specs=[VM] * 2,
        out_shape=[jax.ShapeDtypeStruct((2, s, c, n), F32), jax.ShapeDtypeStruct((s, 6, c, LANES), F32)],
        scratch_shapes=[pltpu.VMEM((2, c, n), BF)],
        compiler_params=params(8), cost_estimate=cost(5),
    )(weight, near, far)


def stats_kernel(me_ref, live_ref, owner_ref, slot_ref, weight_ref, gain_ref, bias_ref, found_ref,
                 own_ref, one_ref, three_ref, two_ref, note_ref, edge_ref, norm_ref, table):
    c = own_ref.shape[3]
    n = 2 * 64 * 64
    lane = lane_ids(c)
    side = (lane + 1) % 64 < 2
    me = me_ref[0]
    for k, ref in enumerate((own_ref, one_ref, two_ref, three_ref)):
        table[k] = ref[...]
    weight = tap_rows(weight_ref[...])
    gain_col = column(gain_ref[...])
    bias_col = column(bias_ref[...])
    note = jnp.zeros((c, LANES), F32)
    edges, sums = [], []

    def pick(t, b, e):
        return lax.rem(me - owner_ref[t, e, 0, b] + 4, 4), slot_ref[t, e, b]

    for b in range(SLOTS):
        south, north, west, east = pick(0, b, 1), pick(0, b, 0), pick(1, b, 0), pick(1, b, 1)
        total = jnp.zeros((c, LANES), F32)
        square = found_ref[b, 0]
        base = found_ref[b, 1]
        for q in range(2):
            rows = jnp.where(lane < 64, table[south[0], q, south[1], 0], table[north[0], q, north[1], 0])
            cols = jnp.where(lane % 2 == 0, table[west[0], q, west[1], 1],
                             roll(table[east[0], q, east[1], 1], -2))
            if q == 1:
                note_ref[2 * b] = rows
                note_ref[2 * b + 1] = cols
            top, bottom, strip = edge_terms(rows, cols, weight)
            edges.append((top, bottom, strip))
            corner = (jnp.where((lane == 0) | (lane == 63), top, 0.0)
                      + jnp.where((lane == 126) | (lane == 61), roll(bottom, 62), 0.0))
            col_off = found_ref[b, 2 + q] + strip + corner - base
            row_off = jnp.where(side, 0.0, found_ref[b, 4 + q] + top + bottom - base)
            total += col_off + row_off
            square += col_off * col_off + row_off * row_off
        sums.append((base, jnp.sum(total, axis=1, keepdims=True), jnp.sum(square, axis=1, keepdims=True)))
    for b, (base, total, square) in enumerate(sums):
        shift = total * (1.0 / n)
        var = square * (1.0 / n) - shift * shift
        live = jnp.where(live_ref[0, b] > 0, 1.0, 0.0)
        gain = lax.rsqrt(jnp.maximum(var, 0.0) + 1e-05) * gain_col * live
        for k, value in enumerate((base + shift, jnp.broadcast_to(gain, (c, LANES)),
                                   jnp.broadcast_to(bias_col * live, (c, LANES)))):
            norm_ref[b, k] = value
            note = jnp.where(lane == 3 * b + k, value, note)
    for b in range(SLOTS):
        for q in range(2):
            for k, term in enumerate(edges[2 * b + q]):
                edge_ref[b, q, k] = term
    for k in range(3):
        part = note.astype(BF)
        note_ref[2 * SLOTS + k] = part
        note = note - part.astype(F32)


def stats(me, live, owner, slot, weight, gain, bias, found, strips):
    s, _, c, _ = found.shape
    return pl.pallas_call(
        stats_kernel, name="stats",
        in_specs=[SM] * 4 + [VM] * 8, out_specs=[VM] * 3,
        out_shape=[jax.ShapeDtypeStruct((2 * s + 3, c, LANES), BF), jax.ShapeDtypeStruct((s, 2, 3, c, LANES), F32),
                   jax.ShapeDtypeStruct((s, 3, c, LANES), F32)],
        scratch_shapes=[pltpu.VMEM((4,) + strips[0].shape, BF)],
        compiler_params=params(8), cost_estimate=cost(0),
    )(me, live, owner, slot, weight, gain, bias, found, *strips)


def activate(plane_ref, edge_ref, norm_ref, q, b, store):
    tiles = plane_ref.shape[3] // LANES
    mean, gain, bias = (norm_ref[b, k] for k in range(3))
    terms = [edge_ref[b, q, k] for k in range(3)]
    for t in range(tiles):
        at = slice(t * LANES, (t + 1) * LANES)
        value = with_edges(plane_ref[q, b, :, at], t, tiles, terms) - mean
        store(at, jnp.maximum(value * gain + bias, 0.0).astype(BF))


def near_kernel(plane_ref, edge_ref, norm_ref, near_ref):
    for b in range(SLOTS):
        def store(at, value):
            near_ref[b, :, at] = value
        activate(plane_ref, edge_ref, norm_ref, 0, b, store)


def near_layer(plane, edge, norm):
    _, s, c, n = plane.shape
    return pl.pallas_call(
        near_kernel, name="near",
        in_specs=[VM] * 3, out_specs=VM,
        out_shape=jax.ShapeDtypeStruct((s, c, n), BF),
        compiler_params=params(4), cost_estimate=cost(0),
    )(plane, edge, norm)


def depth_matrix(side, depth):
    c = depth.shape[0]
    k = lax.broadcasted_iota(jnp.int32, (3 * c, 4 * c), 0)
    j = lax.broadcasted_iota(jnp.int32, (3 * c, 4 * c), 1)
    oi = lax.broadcasted_iota(jnp.int32, (2 * c, c), 0)
    oj = lax.broadcasted_iota(jnp.int32, (2 * c, c), 1)
    total = jnp.zeros((2 * c, 4 * c), F32)
    for z in range(2):
        layer = k // c + z
        place = jnp.where(side > 0, layer, 3 - layer) * c + k % c
        spread = jnp.where(j == place, 1.0, 0.0).astype(BF)
        part = jnp.dot(depth, spread, preferred_element_type=F32).astype(BF)
        pick = jnp.where(oi == 2 * oj + z, 1.0, 0.0).astype(BF)
        total += jnp.dot(pick, part, preferred_element_type=F32)
    return total.astype(BF)


def inner_kernel(side_ref, weight_ref, depth_ref, kept_ref, raw_ref, near_ref, own_ref, edge_ref, norm_ref,
                 plane_ref, part_ref, matrix_ref, act, stack):
    c, n = near_ref.shape[1:]
    depth = depth_matrix(side_ref[0], depth_ref[...])
    matrix_ref[...] = jnp.concatenate([depth[:, :c], depth[:, 3 * c:]], axis=1)
    mine = depth[:, c:3 * c]
    weight = tap_rows(weight_ref[...])
    wide = 512
    for b in range(SLOTS):
        def store(at, value):
            act[:, at] = value
        activate(own_ref, edge_ref, norm_ref, 1, b, store)
        for w in range(n // wide):
            at = slice(w * wide, (w + 1) * wide)
            both = jnp.concatenate([near_ref[b, :, at], act[:, at]], axis=0)
            part_ref[b, :, at] = (jnp.dot(mine, both, preferred_element_type=F32)
                                  + kept_ref[b, :, :, at].reshape(2 * c, wide).astype(F32))

        def emit(t, value):
            plane_ref[b, :, t * LANES:(t + 1) * LANES] = value
        conv_layer(lambda at: raw_ref[b, :, at], weight, stack, emit)


def inner(side, weight, depth, kept, raw, near, plane, edge, norm):
    s, c, n = near.shape
    return pl.pallas_call(
        inner_kernel, name="inner",
        in_specs=[SM] + [VM] * 8, out_specs=[VM] * 3,
        out_shape=[jax.ShapeDtypeStruct((s, c, n), F32), jax.ShapeDtypeStruct((s, 2 * c, n), F32),
                   jax.ShapeDtypeStruct((2 * c, 2 * c), BF)],
        scratch_shapes=[pltpu.VMEM((c, n), BF), pltpu.VMEM((2, c, n), BF)],
        compiler_params=params(8), cost_estimate=cost(100),
    )(side, weight, depth, kept, raw, near, plane, edge, norm)


def final_kernel(live_ref, weight_ref, matrix_ref, plane_ref, part_ref, note_ref, near_in_ref, out_ref, stack, done, edge, norm, sems):
    c, n = near_in_ref.shape[1:]
    tiles = n // LANES
    weight = tap_rows(weight_ref[...])
    matrix = matrix_ref[...]
    stats = note_ref[2 * SLOTS].astype(F32) + note_ref[2 * SLOTS + 1].astype(F32) + note_ref[2 * SLOTS + 2].astype(F32)
    wide = 512
    copies = []
    for b in range(SLOTS):
        for k, term in enumerate(edge_terms(note_ref[2 * b], note_ref[2 * b + 1], weight)):
            edge[b, k] = term
        for k in range(3):
            norm[b, k] = jnp.broadcast_to(stats[:, 3 * b + k:3 * b + k + 1], (c, LANES))
    for b in range(SLOTS):
        mean, gain, bias = (norm[b, k] for k in range(3))
        terms = [edge[b, k] for k in range(3)]
        for t in range(tiles):
            at = slice(t * LANES, (t + 1) * LANES)
            value = with_edges(plane_ref[b, :, at], t, tiles, terms) - mean
            stack[:, at] = jnp.maximum(value * gain + bias, 0.0).astype(BF)
        live = jnp.where(live_ref[0, b] > 0, 1.0, 0.0)
        for w in range(n // wide):
            at = slice(w * wide, (w + 1) * wide)
            both = jnp.concatenate([near_in_ref[b, :, at], stack[:, at]], axis=0)
            mixed = jnp.dot(matrix, both, preferred_element_type=F32)
            done[b, :, :, at] = ((part_ref[b, :, at] + mixed) * live).astype(BF).reshape(c, 2, wide)
        copies.append(pltpu.make_async_copy(done.at[b], out_ref.at[0, b], sems.at[b]))
        copies[-1].start()
    for copy in copies:
        copy.wait()


def final(live, weight, matrix, plane, part, note, near_in):
    s, c, n = near_in.shape
    return pl.pallas_call(
        final_kernel, name="final",
        in_specs=[SM] + [VM] * 6, out_specs=HB,
        out_shape=jax.ShapeDtypeStruct((1, s, c, 2, n), BF),
        scratch_shapes=[pltpu.VMEM((c, n), BF), pltpu.VMEM((s, c, 2, n), BF),
                        pltpu.VMEM((s, 3, c, LANES), F32), pltpu.VMEM((s, 3, c, LANES), F32), pltpu.SemaphoreType.DMA((SLOTS,))],
        compiler_params=params(12), cost_estimate=cost(2),
    )(live, weight, matrix, plane, part, note, near_in)


def swap(value, axis, first):
    count = lax.axis_size(axis)
    pairs = []
    for i in range(first, count - 1, 2):
        pairs += [(i, i + 1), (i + 1, i)]
    return lax.ppermute(value, axis, pairs)


def ring(value, axis, steps):
    count = lax.axis_size(axis)
    return lax.ppermute(value, axis, [(i, (i + steps) % count) for i in range(count)])


def body(volume, tissue, face_owner, face_slot, plane_weight, depth_weight, norm_gain, norm_bias):
    owner = jnp.transpose(face_owner, (0, 2, 3, 1))
    slot = jnp.transpose(face_slot, (0, 2, 1))
    gain = norm_gain.reshape(1, -1)
    bias = norm_bias.reshape(1, -1)
    me = lax.axis_index("blk").reshape(1)
    side = (lax.axis_index("slab") % 2).reshape(1)
    near, far, strips, kept = split(side, me, volume, tissue)
    raw = swap(far, "slab", 1)
    one, three, two = (ring(strips, "blk", k) for k in (1, 3, 2))
    strips = [strips, one, three, two]
    plane, found = bulk(plane_weight, near, far)
    note, edge, norm = stats(me, tissue, owner, slot, plane_weight, gain, bias, found, strips)
    note_in = swap(note, "slab", 1)
    near_act = near_layer(plane, edge, norm)
    near_in = swap(near_act, "slab", 0)
    far_plane, part, matrix = inner(side, plane_weight, depth_weight, kept, raw, near_act, plane, edge, norm)
    return final(tissue, plane_weight, matrix, far_plane, part, note_in, near_in)


def solution(mesh):
    return jax.shard_map(
        body,
        mesh=mesh,
        in_specs=(
            P("slab", "blk", None, None, None),
            P("slab", "blk"),
            P(None, "blk", None, None),
            P(None, "blk", None),
            P(),
            P(),
            P(),
            P(),
        ),
        out_specs=P("slab", "blk", None, None, None),
        check_vma=False,
    )
```

```python
import functools
import jax
import jax.numpy as jnp
from jax import lax
from jax.sharding import PartitionSpec as P
import jax.experimental.pallas as pl
import jax.experimental.pallas.tpu as pltpu

LANES = 128
SLOTS = 3
BF = jnp.bfloat16
F32 = jnp.float32
VM = pl.BlockSpec(memory_space=pltpu.VMEM)
SM = pl.BlockSpec(memory_space=pltpu.SMEM)
HB = pl.BlockSpec(memory_space=pltpu.HBM)


def lane_ids(rows):
    return lax.broadcasted_iota(jnp.int32, (rows, LANES), 1)


def roll(x, k):
    return pltpu.roll(x, k % LANES, 1)


def params(mib):
    return pltpu.CompilerParams(vmem_limit_bytes=mib * 2**20)


def cost(us):
    return pl.CostEstimate(flops=us * 1_000_000_000, bytes_accessed=us * 1_000_000, transcendentals=0)


def split_kernel(side_ref, me_ref, vol_ref, live_ref, near_ref, far_ref, strip_ref, kept_ref, live_s, sems, live_sem):
    c, n = near_ref.shape[1:]
    copies = [pltpu.make_async_copy(vol_ref.at[0, b], kept_ref.at[b], sems.at[b]) for b in range(SLOTS)]
    for copy in copies:
        copy.start()
    lives = pltpu.make_async_copy(live_ref, live_s, live_sem)
    lives.start()
    side = side_ref[0]
    i = lax.broadcasted_iota(jnp.int32, (2 * c, 2 * c), 0)
    j = lax.broadcasted_iota(jnp.int32, (2 * c, 2 * c), 1)
    order = jnp.where(j == jnp.where(i < c, 2 * i + 1 - side, 2 * (i - c) + side), 1.0, 0.0).astype(BF)
    lane = lane_ids(2 * c)
    edge = (lane + 1) % 64 < 2
    zero = jnp.zeros((2 * c, LANES), BF)
    lives.wait()
    for b in range(SLOTS):
        copies[b].wait()
        x = kept_ref[b].reshape(2 * c, n)
        d = jnp.dot(order, x, preferred_element_type=F32).astype(BF)
        near_ref[b] = d[:c]
        far_ref[b] = d[c:]
        live = jnp.where(live_s[0, b] > 0, 1.0, 0.0).astype(BF)
        rows = jnp.where(lane < 64, d[:, :LANES], d[:, n - LANES:])
        cols = zero
        for t in range(n // LANES):
            tile = jnp.where(edge, d[:, t * LANES:(t + 1) * LANES], zero)
            cols += roll(tile, 2 * t + 65)
        rows = rows * live
        cols = cols * live
        for q in range(2):
            strip_ref[q, b, 0] = rows[q * c:(q + 1) * c]
            strip_ref[q, b, 1] = cols[q * c:(q + 1) * c]


def split(side, me, vol, tissue):
    _, s, c, z, n = vol.shape
    return pl.pallas_call(
        split_kernel, name="split",
        in_specs=[SM, SM, HB, HB], out_specs=[VM] * 4,
        out_shape=[jax.ShapeDtypeStruct((s, c, n), BF)] * 2
        + [jax.ShapeDtypeStruct((2, s, 2, c, LANES), BF),
           jax.ShapeDtypeStruct((s, c, z, n), BF)],
        scratch_shapes=[pltpu.SMEM((1, s), jnp.int32), pltpu.SemaphoreType.DMA((SLOTS,)), pltpu.SemaphoreType.DMA],
        compiler_params=params(24),
    )(side, me, pltpu.with_memory_space_constraint(vol, pltpu.HBM), pltpu.with_memory_space_constraint(tissue, pltpu.HBM))


def conv_layer(x_at, weight, stack, emit):
    c, n = stack.shape[1:]
    tiles = n // LANES
    lane = lane_ids(c)
    zero = jnp.zeros((c, LANES), BF)
    low = lane < 64
    for t in range(tiles):
        at = slice(t * LANES, (t + 1) * LANES)
        tile = x_at(at)
        stack[0, :, at] = jnp.where(lane % 64 == 0, zero, roll(tile, 1))
        stack[1, :, at] = jnp.where(lane % 64 == 63, zero, roll(tile, -1))
    above = jnp.zeros((c, LANES), F32)
    middle = turned = None
    for pair in range(tiles // 2):
        at = slice(pair * 2 * LANES, (pair + 1) * 2 * LANES)
        taps = jnp.concatenate([stack[0, :, at], x_at(at), stack[1, :, at]], axis=0)
        u = jnp.dot(weight, taps, preferred_element_type=F32)
        for h in range(2):
            part = u[:, h * LANES:(h + 1) * LANES]
            turn = roll(above + part[2 * c:], 64)
            t = 2 * pair + h
            if t:
                emit(t - 1, middle + jnp.where(low, turned, turn))
            above, middle, turned = part[:c], part[c:2 * c], turn
    emit(tiles - 1, middle + jnp.where(low, turned, roll(above, 64)))


def edge_terms(rows, cols, weight):
    c = rows.shape[0]
    lane = lane_ids(c)
    zero = jnp.zeros((c, LANES), BF)
    low = lane < 64
    even = lane % 2 == 0
    row_taps = jnp.concatenate([jnp.where(lane % 64 == 0, zero, roll(rows, 1)), rows,
                                jnp.where(lane % 64 == 63, zero, roll(rows, -1))], axis=0)
    col_taps = jnp.concatenate([jnp.where(even, cols, zero), zero, jnp.where(even, zero, cols)], axis=0)
    u = jnp.dot(weight, jnp.concatenate([row_taps, col_taps], axis=1), preferred_element_type=F32)
    top = jnp.where(low, roll(u[:c, :LANES], 64), 0.0)
    bottom = jnp.where(low, 0.0, roll(u[2 * c:, :LANES], 64))
    v = u[:, LANES:]
    place = jnp.where(even, lane, (lane + 65) % LANES)
    upper = jnp.where(place < 64, jnp.where(place == 0, 0.0, roll(v[:c], 66)), roll(v[:c], 64))
    lower = jnp.where(place < 64, roll(v[2 * c:], 64), jnp.where(place == 126, 0.0, roll(v[2 * c:], 62)))
    return top, bottom, v[c:2 * c] + upper + lower


def with_edges(value, t, tiles, terms):
    top, bottom, strip = terms
    lane = lane_ids(value.shape[0])
    value = value + jnp.where((lane + 1) % 64 < 2, roll(strip, -2 * t), 0.0)
    if t == 0:
        value = value + top
    if t == tiles - 1:
        value = value + bottom
    return value


def tap_rows(weight):
    width = weight.shape[1] // 3
    return jnp.concatenate([weight[:, a * width:(a + 1) * width] for a in range(3)], axis=0)


def column(row):
    c = row.shape[1]
    i = lax.broadcasted_iota(jnp.int32, (c, c), 0)
    j = lax.broadcasted_iota(jnp.int32, (c, c), 1)
    return jnp.sum(jnp.where(i == j, jnp.broadcast_to(row, (c, c)), 0.0), axis=1, keepdims=True)


def bulk_kernel(weight_ref, near_ref, far_ref, plane_ref, found_ref, stack):
    c, n = near_ref.shape[1:]
    tiles = n // LANES
    weight = tap_rows(weight_ref[...])
    lane = lane_ids(c)
    edge = (lane + 1) % 64 < 2
    low = lane < 64
    inside = 2 * (n - 4 * 64 + 4)

    def within(t, value):
        if t == 0:
            value = jnp.where(low, 0.0, value)
        if t == tiles - 1:
            value = jnp.where(low, value, 0.0)
        return value

    for b in range(SLOTS):
        total = [jnp.zeros((c, LANES), F32)]
        for q, ref in enumerate((near_ref, far_ref)):
            def emit(t, value):
                plane_ref[q, b, :, t * LANES:(t + 1) * LANES] = value
                total[0] += within(t, jnp.where(edge, 0.0, value))
            conv_layer(lambda at: ref[b, :, at], weight, stack, emit)
        mean = jnp.sum(total[0], axis=1, keepdims=True) * (1.0 / inside)
        mean = jnp.broadcast_to(mean, (c, LANES))
        square = jnp.zeros((c, LANES), F32)
        for q in range(2):
            strip = jnp.zeros((c, LANES), F32)
            for t in range(tiles):
                off = plane_ref[q, b, :, t * LANES:(t + 1) * LANES] - mean
                side = jnp.where(edge, off, 0.0)
                strip += roll(side, 2 * t)
                inner = within(t, off - side)
                square += inner * inner
            rows = jnp.where(low, plane_ref[q, b, :, :LANES], plane_ref[q, b, :, n - LANES:]) - mean
            found_ref[b, 2 + q] = strip
            found_ref[b, 4 + q] = jnp.where(edge, 0.0, rows)
        found_ref[b, 0] = square
        found_ref[b, 1] = mean


def bulk(weight, near, far):
    s, c, n = near.shape
    return pl.pallas_call(
        bulk_kernel, name="bulk",
        in_specs=[VM] * 3, out_specs=[VM] * 2,
        out_shape=[jax.ShapeDtypeStruct((2, s, c, n), F32), jax.ShapeDtypeStruct((s, 6, c, LANES), F32)],
        scratch_shapes=[pltpu.VMEM((2, c, n), BF)],
        compiler_params=params(8), cost_estimate=cost(5),
    )(weight, near, far)


def stats_kernel(me_ref, live_ref, owner_ref, slot_ref, weight_ref, gain_ref, bias_ref, found_ref,
                 own_ref, one_ref, three_ref, two_ref, note_ref, edge_ref, norm_ref, table):
    c = own_ref.shape[3]
    n = 2 * 64 * 64
    lane = lane_ids(c)
    side = (lane + 1) % 64 < 2
    me = me_ref[0]
    for k, ref in enumerate((own_ref, one_ref, two_ref, three_ref)):
        table[k] = ref[...]
    weight = tap_rows(weight_ref[...])
    gain_col = column(gain_ref[...])
    bias_col = column(bias_ref[...])
    note = jnp.zeros((c, LANES), F32)
    edges, sums = [], []

    def pick(t, b, e):
        return lax.rem(me - owner_ref[t, e, 0, b] + 4, 4), slot_ref[t, e, b]

    for b in range(SLOTS):
        south, north, west, east = pick(0, b, 1), pick(0, b, 0), pick(1, b, 0), pick(1, b, 1)
        total = jnp.zeros((c, LANES), F32)
        square = found_ref[b, 0]
        base = found_ref[b, 1]
        for q in range(2):
            rows = jnp.where(lane < 64, table[south[0], q, south[1], 0], table[north[0], q, north[1], 0])
            cols = jnp.where(lane % 2 == 0, table[west[0], q, west[1], 1],
                             roll(table[east[0], q, east[1], 1], -2))
            if q == 1:
                note_ref[2 * b] = rows
                note_ref[2 * b + 1] = cols
            top, bottom, strip = edge_terms(rows, cols, weight)
            edges.append((top, bottom, strip))
            corner = (jnp.where((lane == 0) | (lane == 63), top, 0.0)
                      + jnp.where((lane == 126) | (lane == 61), roll(bottom, 62), 0.0))
            col_off = found_ref[b, 2 + q] + strip + corner
            row_off = jnp.where(side, 0.0, found_ref[b, 4 + q] + top + bottom)
            total += col_off + row_off
            square += col_off * col_off + row_off * row_off
        sums.append((base, jnp.sum(total, axis=1, keepdims=True), jnp.sum(square, axis=1, keepdims=True)))
    for b, (base, total, square) in enumerate(sums):
        shift = total * (1.0 / n)
        var = square * (1.0 / n) - shift * shift
        live = jnp.where(live_ref[0, b] > 0, 1.0, 0.0)
        gain = lax.rsqrt(jnp.maximum(var, 0.0) + 1e-05) * gain_col * live
        for k, value in enumerate((base + shift, jnp.broadcast_to(gain, (c, LANES)),
                                   jnp.broadcast_to(bias_col * live, (c, LANES)))):
            norm_ref[b, k] = value
            note = jnp.where(lane == 3 * b + k, value, note)
    for b in range(SLOTS):
        for q in range(2):
            for k, term in enumerate(edges[2 * b + q]):
                edge_ref[b, q, k] = term
    packed = jnp.zeros((c, LANES), F32)
    for k in range(3):
        part = note.astype(BF).astype(F32)
        packed += roll(part, 3 * SLOTS * k)
        note = note - part
    note_ref[2 * SLOTS] = packed.astype(BF)


def stats(me, live, owner, slot, weight, gain, bias, found, strips):
    s, _, c, _ = found.shape
    return pl.pallas_call(
        stats_kernel, name="stats",
        in_specs=[SM] * 4 + [VM] * 8, out_specs=[VM] * 3,
        out_shape=[jax.ShapeDtypeStruct((2 * s + 1, c, LANES), BF), jax.ShapeDtypeStruct((s, 2, 3, c, LANES), F32),
                   jax.ShapeDtypeStruct((s, 3, c, LANES), F32)],
        scratch_shapes=[pltpu.VMEM((4,) + strips[0].shape, BF)],
        compiler_params=params(8), cost_estimate=cost(0),
    )(me, live, owner, slot, weight, gain, bias, found, *strips)


def activate(plane_ref, edge_ref, norm_ref, q, b, store):
    tiles = plane_ref.shape[3] // LANES
    mean, gain, bias = (norm_ref[b, k] for k in range(3))
    terms = [edge_ref[b, q, k] for k in range(3)]
    for t in range(tiles):
        at = slice(t * LANES, (t + 1) * LANES)
        value = with_edges(plane_ref[q, b, :, at], t, tiles, terms) - mean
        store(at, jnp.maximum(value * gain + bias, 0.0).astype(BF))


def near_kernel(plane_ref, edge_ref, norm_ref, near_ref):
    for b in range(SLOTS):
        def store(at, value):
            near_ref[b, :, at] = value
        activate(plane_ref, edge_ref, norm_ref, 0, b, store)


def near_layer(plane, edge, norm):
    _, s, c, n = plane.shape
    return pl.pallas_call(
        near_kernel, name="near",
        in_specs=[VM] * 3, out_specs=VM,
        out_shape=jax.ShapeDtypeStruct((s, c, n), BF),
        compiler_params=params(4), cost_estimate=cost(0),
    )(plane, edge, norm)


def depth_matrix(side, depth):
    c = depth.shape[0]
    k = lax.broadcasted_iota(jnp.int32, (3 * c, 4 * c), 0)
    j = lax.broadcasted_iota(jnp.int32, (3 * c, 4 * c), 1)
    oi = lax.broadcasted_iota(jnp.int32, (2 * c, c), 0)
    oj = lax.broadcasted_iota(jnp.int32, (2 * c, c), 1)
    total = jnp.zeros((2 * c, 4 * c), F32)
    for z in range(2):
        layer = k // c + z
        place = jnp.where(side > 0, layer, 3 - layer) * c + k % c
        spread = jnp.where(j == place, 1.0, 0.0).astype(BF)
        part = jnp.dot(depth, spread, preferred_element_type=F32).astype(BF)
        pick = jnp.where(oi == 2 * oj + z, 1.0, 0.0).astype(BF)
        total += jnp.dot(pick, part, preferred_element_type=F32)
    return total.astype(BF)


def inner_kernel(side_ref, weight_ref, depth_ref, kept_ref, raw_ref, near_ref, own_ref, edge_ref, norm_ref,
                 plane_ref, part_ref, matrix_ref, act, stack):
    c, n = near_ref.shape[1:]
    depth = depth_matrix(side_ref[0], depth_ref[...])
    matrix_ref[...] = jnp.concatenate([depth[:, :c], depth[:, 3 * c:]], axis=1)
    mine = depth[:, c:3 * c]
    weight = tap_rows(weight_ref[...])
    wide = 512
    for b in range(SLOTS):
        def store(at, value):
            act[:, at] = value
        activate(own_ref, edge_ref, norm_ref, 1, b, store)
        for w in range(n // wide):
            at = slice(w * wide, (w + 1) * wide)
            both = jnp.concatenate([near_ref[b, :, at], act[:, at]], axis=0)
            part_ref[b, :, at] = (jnp.dot(mine, both, preferred_element_type=F32)
                                  + kept_ref[b, :, :, at].reshape(2 * c, wide).astype(F32))

        def emit(t, value):
            plane_ref[b, :, t * LANES:(t + 1) * LANES] = value
        conv_layer(lambda at: raw_ref[b, :, at], weight, stack, emit)


def inner(side, weight, depth, kept, raw, near, plane, edge, norm):
    s, c, n = near.shape
    return pl.pallas_call(
        inner_kernel, name="inner",
        in_specs=[SM] + [VM] * 8, out_specs=[VM] * 3,
        out_shape=[jax.ShapeDtypeStruct((s, c, n), F32), jax.ShapeDtypeStruct((s, 2 * c, n), F32),
                   jax.ShapeDtypeStruct((2 * c, 2 * c), BF)],
        scratch_shapes=[pltpu.VMEM((c, n), BF), pltpu.VMEM((2, c, n), BF)],
        compiler_params=params(8), cost_estimate=cost(100),
    )(side, weight, depth, kept, raw, near, plane, edge, norm)


def final_kernel(live_ref, weight_ref, matrix_ref, plane_ref, part_ref, note_ref, near_in_ref, out_ref, stack, done, edge, norm, sems):
    c, n = near_in_ref.shape[1:]
    tiles = n // LANES
    weight = tap_rows(weight_ref[...])
    matrix = matrix_ref[...]
    stats = note_ref[2 * SLOTS].astype(F32)
    stats = stats + roll(stats, -3 * SLOTS) + roll(stats, -6 * SLOTS)
    wide = 512
    copies = []
    for b in range(SLOTS):
        for k, term in enumerate(edge_terms(note_ref[2 * b], note_ref[2 * b + 1], weight)):
            edge[b, k] = term
        for k in range(3):
            norm[b, k] = jnp.broadcast_to(stats[:, 3 * b + k:3 * b + k + 1], (c, LANES))
    for b in range(SLOTS):
        mean, gain, bias = (norm[b, k] for k in range(3))
        terms = [edge[b, k] for k in range(3)]
        for t in range(tiles):
            at = slice(t * LANES, (t + 1) * LANES)
            value = with_edges(plane_ref[b, :, at], t, tiles, terms) - mean
            stack[:, at] = jnp.maximum(value * gain + bias, 0.0).astype(BF)
        live = jnp.where(live_ref[0, b] > 0, 1.0, 0.0)
        for w in range(n // wide):
            at = slice(w * wide, (w + 1) * wide)
            both = jnp.concatenate([near_in_ref[b, :, at], stack[:, at]], axis=0)
            mixed = jnp.dot(matrix, both, preferred_element_type=F32)
            done[b, :, :, at] = ((part_ref[b, :, at] + mixed) * live).astype(BF).reshape(c, 2, wide)
            if w % 2:
                lanes = pl.ds((w - 1) * wide, 2 * wide)
                copies.append(pltpu.make_async_copy(done.at[b, :, :, lanes], out_ref.at[0, b, :, :, lanes],
                                                    sems.at[len(copies)]))
                copies[-1].start()
    for copy in copies:
        copy.wait()


def final(live, weight, matrix, plane, part, note, near_in):
    s, c, n = near_in.shape
    return pl.pallas_call(
        final_kernel, name="final",
        in_specs=[SM] + [VM] * 6, out_specs=HB,
        out_shape=jax.ShapeDtypeStruct((1, s, c, 2, n), BF),
        scratch_shapes=[pltpu.VMEM((c, n), BF), pltpu.VMEM((s, c, 2, n), BF),
                        pltpu.VMEM((s, 3, c, LANES), F32), pltpu.VMEM((s, 3, c, LANES), F32),
                        pltpu.SemaphoreType.DMA((n // 1024 * SLOTS,))],
        compiler_params=params(12), cost_estimate=cost(2),
    )(live, weight, matrix, plane, part, note, near_in)


def swap(value, axis, first):
    count = lax.axis_size(axis)
    pairs = []
    for i in range(first, count - 1, 2):
        pairs += [(i, i + 1), (i + 1, i)]
    return lax.ppermute(value, axis, pairs)


def ring(value, axis, steps):
    count = lax.axis_size(axis)
    return lax.ppermute(value, axis, [(i, (i + steps) % count) for i in range(count)])


def body(volume, tissue, face_owner, face_slot, plane_weight, depth_weight, norm_gain, norm_bias):
    owner = jnp.transpose(face_owner, (0, 2, 3, 1))
    slot = jnp.transpose(face_slot, (0, 2, 1))
    gain = norm_gain.reshape(1, -1)
    bias = norm_bias.reshape(1, -1)
    me = lax.axis_index("blk").reshape(1)
    side = (lax.axis_index("slab") % 2).reshape(1)
    near, far, strips, kept = split(side, me, volume, tissue)
    raw = swap(far, "slab", 1)
    one, three, two = (ring(strips, "blk", k) for k in (1, 3, 2))
    strips = [strips, one, three, two]
    plane, found = bulk(plane_weight, near, far)
    note, edge, norm = stats(me, tissue, owner, slot, plane_weight, gain, bias, found, strips)
    note_in = swap(note, "slab", 1)
    near_act = near_layer(plane, edge, norm)
    near_in = swap(near_act, "slab", 0)
    far_plane, part, matrix = inner(side, plane_weight, depth_weight, kept, raw, near_act, plane, edge, norm)
    return final(tissue, plane_weight, matrix, far_plane, part, note_in, near_in)


def solution(mesh):
    return jax.shard_map(
        body,
        mesh=mesh,
        in_specs=(
            P("slab", "blk", None, None, None),
            P("slab", "blk"),
            P(None, "blk", None, None),
            P(None, "blk", None),
            P(),
            P(),
            P(),
            P(),
        ),
        out_specs=P("slab", "blk", None, None, None),
        check_vma=False,
    )
```

```python
import functools
import jax
import jax.numpy as jnp
from jax import lax
from jax.sharding import PartitionSpec as P
import jax.experimental.pallas as pl
import jax.experimental.pallas.tpu as pltpu

LANES = 128
SLOTS = 3
BF = jnp.bfloat16
F32 = jnp.float32
VM = pl.BlockSpec(memory_space=pltpu.VMEM)
SM = pl.BlockSpec(memory_space=pltpu.SMEM)
HB = pl.BlockSpec(memory_space=pltpu.HBM)


def lane_ids(rows):
    return lax.broadcasted_iota(jnp.int32, (rows, LANES), 1)


def roll(x, k):
    return pltpu.roll(x, k % LANES, 1)


def params(mib):
    return pltpu.CompilerParams(vmem_limit_bytes=mib * 2**20)


def cost(us):
    return pl.CostEstimate(flops=us * 1_000_000_000, bytes_accessed=us * 1_000_000, transcendentals=0)


def split_kernel(side_ref, me_ref, vol_ref, live_ref, near_ref, far_ref, strip_ref, kept_ref, live_s, sems, live_sem):
    c, n = near_ref.shape[1:]
    copies = [pltpu.make_async_copy(vol_ref.at[0, b], kept_ref.at[b], sems.at[b]) for b in range(SLOTS)]
    for copy in copies:
        copy.start()
    lives = pltpu.make_async_copy(live_ref, live_s, live_sem)
    lives.start()
    side = side_ref[0]
    i = lax.broadcasted_iota(jnp.int32, (2 * c, 2 * c), 0)
    j = lax.broadcasted_iota(jnp.int32, (2 * c, 2 * c), 1)
    order = jnp.where(j == jnp.where(i < c, 2 * i + 1 - side, 2 * (i - c) + side), 1.0, 0.0).astype(BF)
    lane = lane_ids(2 * c)
    edge = (lane + 1) % 64 < 2
    zero = jnp.zeros((2 * c, LANES), BF)
    lives.wait()
    for b in range(SLOTS):
        copies[b].wait()
        x = kept_ref[b].reshape(2 * c, n)
        d = jnp.dot(order, x, preferred_element_type=F32).astype(BF)
        near_ref[b] = d[:c]
        far_ref[b] = d[c:]
        live = jnp.where(live_s[0, b] > 0, 1.0, 0.0).astype(BF)
        rows = jnp.where(lane < 64, d[:, :LANES], d[:, n - LANES:])
        cols = zero
        for t in range(n // LANES):
            tile = jnp.where(edge, d[:, t * LANES:(t + 1) * LANES], zero)
            cols += roll(tile, 2 * t + 65)
        rows = rows * live
        cols = cols * live
        for q in range(2):
            strip_ref[q, b, 0] = rows[q * c:(q + 1) * c]
            strip_ref[q, b, 1] = cols[q * c:(q + 1) * c]


def split(side, me, vol, tissue):
    _, s, c, z, n = vol.shape
    return pl.pallas_call(
        split_kernel, name="split",
        in_specs=[SM, SM, HB, HB], out_specs=[VM] * 4,
        out_shape=[jax.ShapeDtypeStruct((s, c, n), BF)] * 2
        + [jax.ShapeDtypeStruct((2, s, 2, c, LANES), BF),
           jax.ShapeDtypeStruct((s, c, z, n), BF)],
        scratch_shapes=[pltpu.SMEM((1, s), jnp.int32), pltpu.SemaphoreType.DMA((SLOTS,)), pltpu.SemaphoreType.DMA],
        compiler_params=params(24),
    )(side, me, pltpu.with_memory_space_constraint(vol, pltpu.HBM), pltpu.with_memory_space_constraint(tissue, pltpu.HBM))


def conv_layer(x_at, weight, stack, emit):
    c, n = stack.shape[1:]
    tiles = n // LANES
    lane = lane_ids(c)
    zero = jnp.zeros((c, LANES), BF)
    low = lane < 64
    for t in range(tiles):
        at = slice(t * LANES, (t + 1) * LANES)
        tile = x_at(at)
        stack[0, :, at] = jnp.where(lane % 64 == 0, zero, roll(tile, 1))
        stack[1, :, at] = jnp.where(lane % 64 == 63, zero, roll(tile, -1))
    above = jnp.zeros((c, LANES), F32)
    middle = turned = None
    for pair in range(tiles // 2):
        at = slice(pair * 2 * LANES, (pair + 1) * 2 * LANES)
        taps = jnp.concatenate([stack[0, :, at], x_at(at), stack[1, :, at]], axis=0)
        u = jnp.dot(weight, taps, preferred_element_type=F32)
        for h in range(2):
            part = u[:, h * LANES:(h + 1) * LANES]
            turn = roll(above + part[2 * c:], 64)
            t = 2 * pair + h
            if t:
                emit(t - 1, middle + jnp.where(low, turned, turn))
            above, middle, turned = part[:c], part[c:2 * c], turn
    emit(tiles - 1, middle + jnp.where(low, turned, roll(above, 64)))


def edge_terms(rows, cols, weight):
    c = rows.shape[0]
    lane = lane_ids(c)
    zero = jnp.zeros((c, LANES), BF)
    low = lane < 64
    even = lane % 2 == 0
    row_taps = jnp.concatenate([jnp.where(lane % 64 == 0, zero, roll(rows, 1)), rows,
                                jnp.where(lane % 64 == 63, zero, roll(rows, -1))], axis=0)
    col_taps = jnp.concatenate([jnp.where(even, cols, zero), zero, jnp.where(even, zero, cols)], axis=0)
    u = jnp.dot(weight, jnp.concatenate([row_taps, col_taps], axis=1), preferred_element_type=F32)
    top = jnp.where(low, roll(u[:c, :LANES], 64), 0.0)
    bottom = jnp.where(low, 0.0, roll(u[2 * c:, :LANES], 64))
    v = u[:, LANES:]
    place = jnp.where(even, lane, (lane + 65) % LANES)
    upper = jnp.where(place < 64, jnp.where(place == 0, 0.0, roll(v[:c], 66)), roll(v[:c], 64))
    lower = jnp.where(place < 64, roll(v[2 * c:], 64), jnp.where(place == 126, 0.0, roll(v[2 * c:], 62)))
    return top, bottom, v[c:2 * c] + upper + lower


def with_edges(value, t, tiles, terms):
    top, bottom, strip = terms
    lane = lane_ids(value.shape[0])
    value = value + jnp.where((lane + 1) % 64 < 2, roll(strip, -2 * t), 0.0)
    if t == 0:
        value = value + top
    if t == tiles - 1:
        value = value + bottom
    return value


def tap_rows(weight):
    width = weight.shape[1] // 3
    return jnp.concatenate([weight[:, a * width:(a + 1) * width] for a in range(3)], axis=0)


def column(row):
    c = row.shape[1]
    i = lax.broadcasted_iota(jnp.int32, (c, c), 0)
    j = lax.broadcasted_iota(jnp.int32, (c, c), 1)
    return jnp.sum(jnp.where(i == j, jnp.broadcast_to(row, (c, c)), 0.0), axis=1, keepdims=True)


def bulk_kernel(weight_ref, near_ref, far_ref, plane_ref, found_ref, taps_ref, stack):
    c, n = near_ref.shape[1:]
    tiles = n // LANES
    weight = tap_rows(weight_ref[...])
    taps_ref[...] = weight
    lane = lane_ids(c)
    edge = (lane + 1) % 64 < 2
    low = lane < 64
    inside = 2 * (n - 4 * 64 + 4)

    def within(t, value):
        if t == 0:
            value = jnp.where(low, 0.0, value)
        if t == tiles - 1:
            value = jnp.where(low, value, 0.0)
        return value

    for b in range(SLOTS):
        total = [jnp.zeros((c, LANES), F32)]
        for q, ref in enumerate((near_ref, far_ref)):
            def emit(t, value):
                plane_ref[q, b, :, t * LANES:(t + 1) * LANES] = value
                total[0] += within(t, jnp.where(edge, 0.0, value))
            conv_layer(lambda at: ref[b, :, at], weight, stack, emit)
        mean = jnp.sum(total[0], axis=1, keepdims=True) * (1.0 / inside)
        mean = jnp.broadcast_to(mean, (c, LANES))
        square = jnp.zeros((c, LANES), F32)
        for q in range(2):
            strip = jnp.zeros((c, LANES), F32)
            for t in range(tiles):
                off = plane_ref[q, b, :, t * LANES:(t + 1) * LANES] - mean
                side = jnp.where(edge, off, 0.0)
                strip += roll(side, 2 * t)
                inner = within(t, off - side)
                square += inner * inner
            rows = jnp.where(low, plane_ref[q, b, :, :LANES], plane_ref[q, b, :, n - LANES:]) - mean
            found_ref[b, 2 + q] = strip
            found_ref[b, 4 + q] = jnp.where(edge, 0.0, rows)
        found_ref[b, 0] = square
        found_ref[b, 1] = mean


def bulk(weight, near, far):
    s, c, n = near.shape
    return pl.pallas_call(
        bulk_kernel, name="bulk",
        in_specs=[VM] * 3, out_specs=[VM] * 3,
        out_shape=[jax.ShapeDtypeStruct((2, s, c, n), F32), jax.ShapeDtypeStruct((s, 6, c, LANES), F32),
                   jax.ShapeDtypeStruct((3 * c, 3 * c), BF)],
        scratch_shapes=[pltpu.VMEM((2, c, n), BF)],
        compiler_params=params(8), cost_estimate=cost(5),
    )(weight, near, far)


def stats_kernel(me_ref, live_ref, owner_ref, slot_ref, weight_ref, gain_ref, bias_ref, found_ref,
                 own_ref, one_ref, three_ref, two_ref, note_ref, edge_ref, norm_ref, table):
    c = own_ref.shape[3]
    n = 2 * 64 * 64
    lane = lane_ids(c)
    side = (lane + 1) % 64 < 2
    me = me_ref[0]
    for k, ref in enumerate((own_ref, one_ref, two_ref, three_ref)):
        table[k] = ref[...]
    weight = weight_ref[...]
    gain_col = column(gain_ref[...])
    bias_col = column(bias_ref[...])
    note = jnp.zeros((c, LANES), F32)
    edges, sums = [], []

    def pick(t, b, e):
        return lax.rem(me - owner_ref[t, e, 0, b] + 4, 4), slot_ref[t, e, b]

    for b in range(SLOTS):
        south, north, west, east = pick(0, b, 1), pick(0, b, 0), pick(1, b, 0), pick(1, b, 1)
        total = jnp.zeros((c, LANES), F32)
        square = found_ref[b, 0]
        base = found_ref[b, 1]
        for q in range(2):
            rows = jnp.where(lane < 64, table[south[0], q, south[1], 0], table[north[0], q, north[1], 0])
            cols = jnp.where(lane % 2 == 0, table[west[0], q, west[1], 1],
                             roll(table[east[0], q, east[1], 1], -2))
            if q == 1:
                note_ref[2 * b] = rows
                note_ref[2 * b + 1] = cols
            top, bottom, strip = edge_terms(rows, cols, weight)
            edges.append((top, bottom, strip))
            corner = (jnp.where((lane == 0) | (lane == 63), top, 0.0)
                      + jnp.where((lane == 126) | (lane == 61), roll(bottom, 62), 0.0))
            col_off = found_ref[b, 2 + q] + strip + corner
            row_off = jnp.where(side, 0.0, found_ref[b, 4 + q] + top + bottom)
            total += col_off + row_off
            square += col_off * col_off + row_off * row_off
        sums.append((base, jnp.sum(total, axis=1, keepdims=True), jnp.sum(square, axis=1, keepdims=True)))
    for b, (base, total, square) in enumerate(sums):
        shift = total * (1.0 / n)
        var = square * (1.0 / n) - shift * shift
        live = jnp.where(live_ref[0, b] > 0, 1.0, 0.0)
        gain = lax.rsqrt(jnp.maximum(var, 0.0) + 1e-05) * gain_col * live
        for k, value in enumerate((base + shift, jnp.broadcast_to(gain, (c, LANES)),
                                   jnp.broadcast_to(bias_col * live, (c, LANES)))):
            norm_ref[b, k] = value
            note = jnp.where(lane == 3 * b + k, value, note)
    for b in range(SLOTS):
        for q in range(2):
            for k, term in enumerate(edges[2 * b + q]):
                edge_ref[b, q, k] = term
    packed = jnp.zeros((c, LANES), F32)
    for k in range(3):
        part = note.astype(BF).astype(F32)
        packed += roll(part, 3 * SLOTS * k)
        note = note - part
    note_ref[2 * SLOTS] = packed.astype(BF)


def stats(me, live, owner, slot, weight, gain, bias, found, strips):
    s, _, c, _ = found.shape
    return pl.pallas_call(
        stats_kernel, name="stats",
        in_specs=[SM] * 4 + [VM] * 8, out_specs=[VM] * 3,
        out_shape=[jax.ShapeDtypeStruct((2 * s + 1, c, LANES), BF), jax.ShapeDtypeStruct((s, 2, 3, c, LANES), F32),
                   jax.ShapeDtypeStruct((s, 3, c, LANES), F32)],
        scratch_shapes=[pltpu.VMEM((4,) + strips[0].shape, BF)],
        compiler_params=params(8), cost_estimate=cost(0),
    )(me, live, owner, slot, weight, gain, bias, found, *strips)


def activate(plane_ref, edge_ref, norm_ref, q, b, store):
    tiles = plane_ref.shape[3] // LANES
    mean, gain, bias = (norm_ref[b, k] for k in range(3))
    terms = [edge_ref[b, q, k] for k in range(3)]
    for t in range(tiles):
        at = slice(t * LANES, (t + 1) * LANES)
        value = with_edges(plane_ref[q, b, :, at], t, tiles, terms) - mean
        store(at, jnp.maximum(value * gain + bias, 0.0).astype(BF))


def near_kernel(plane_ref, edge_ref, norm_ref, near_ref):
    for b in range(SLOTS):
        def store(at, value):
            near_ref[b, :, at] = value
        activate(plane_ref, edge_ref, norm_ref, 0, b, store)


def near_layer(plane, edge, norm):
    _, s, c, n = plane.shape
    return pl.pallas_call(
        near_kernel, name="near",
        in_specs=[VM] * 3, out_specs=VM,
        out_shape=jax.ShapeDtypeStruct((s, c, n), BF),
        compiler_params=params(4), cost_estimate=cost(0),
    )(plane, edge, norm)


def depth_matrix(side, depth):
    c = depth.shape[0]
    k = lax.broadcasted_iota(jnp.int32, (3 * c, 4 * c), 0)
    j = lax.broadcasted_iota(jnp.int32, (3 * c, 4 * c), 1)
    oi = lax.broadcasted_iota(jnp.int32, (2 * c, c), 0)
    oj = lax.broadcasted_iota(jnp.int32, (2 * c, c), 1)
    total = jnp.zeros((2 * c, 4 * c), F32)
    for z in range(2):
        layer = k // c + z
        place = jnp.where(side > 0, layer, 3 - layer) * c + k % c
        spread = jnp.where(j == place, 1.0, 0.0).astype(BF)
        part = jnp.dot(depth, spread, preferred_element_type=F32).astype(BF)
        pick = jnp.where(oi == 2 * oj + z, 1.0, 0.0).astype(BF)
        total += jnp.dot(pick, part, preferred_element_type=F32)
    return total.astype(BF)


def inner_kernel(side_ref, weight_ref, depth_ref, kept_ref, raw_ref, near_ref, own_ref, edge_ref, norm_ref,
                 plane_ref, part_ref, matrix_ref, act, stack):
    c, n = near_ref.shape[1:]
    depth = depth_matrix(side_ref[0], depth_ref[...])
    matrix_ref[...] = jnp.concatenate([depth[:, :c], depth[:, 3 * c:]], axis=1)
    mine = depth[:, c:3 * c]
    weight = weight_ref[...]
    wide = 512
    for b in range(SLOTS):
        def store(at, value):
            act[:, at] = value
        activate(own_ref, edge_ref, norm_ref, 1, b, store)
        for w in range(n // wide):
            at = slice(w * wide, (w + 1) * wide)
            both = jnp.concatenate([near_ref[b, :, at], act[:, at]], axis=0)
            part_ref[b, :, at] = (jnp.dot(mine, both, preferred_element_type=F32)
                                  + kept_ref[b, :, :, at].reshape(2 * c, wide).astype(F32))

        def emit(t, value):
            plane_ref[b, :, t * LANES:(t + 1) * LANES] = value
        conv_layer(lambda at: raw_ref[b, :, at], weight, stack, emit)


def inner(side, weight, depth, kept, raw, near, plane, edge, norm):
    s, c, n = near.shape
    return pl.pallas_call(
        inner_kernel, name="inner",
        in_specs=[SM] + [VM] * 8, out_specs=[VM] * 3,
        out_shape=[jax.ShapeDtypeStruct((s, c, n), F32), jax.ShapeDtypeStruct((s, 2 * c, n), F32),
                   jax.ShapeDtypeStruct((2 * c, 2 * c), BF)],
        scratch_shapes=[pltpu.VMEM((c, n), BF), pltpu.VMEM((2, c, n), BF)],
        compiler_params=params(8), cost_estimate=cost(100),
    )(side, weight, depth, kept, raw, near, plane, edge, norm)


def final_kernel(live_ref, weight_ref, matrix_ref, plane_ref, part_ref, note_ref, near_in_ref, out_ref, stack, done, edge, norm, sems):
    c, n = near_in_ref.shape[1:]
    tiles = n // LANES
    weight = weight_ref[...]
    matrix = matrix_ref[...]
    stats = note_ref[2 * SLOTS].astype(F32)
    stats = stats + roll(stats, -3 * SLOTS) + roll(stats, -6 * SLOTS)
    wide = 512
    copies = []
    for b in range(SLOTS):
        for k, term in enumerate(edge_terms(note_ref[2 * b], note_ref[2 * b + 1], weight)):
            edge[b, k] = term
        for k in range(3):
            norm[b, k] = jnp.broadcast_to(stats[:, 3 * b + k:3 * b + k + 1], (c, LANES))
    for b in range(SLOTS):
        mean, gain, bias = (norm[b, k] for k in range(3))
        terms = [edge[b, k] for k in range(3)]
        for t in range(tiles):
            at = slice(t * LANES, (t + 1) * LANES)
            value = with_edges(plane_ref[b, :, at], t, tiles, terms) - mean
            stack[:, at] = jnp.maximum(value * gain + bias, 0.0).astype(BF)
        live = jnp.where(live_ref[0, b] > 0, 1.0, 0.0).astype(BF)
        for w in range(n // wide):
            at = slice(w * wide, (w + 1) * wide)
            both = jnp.concatenate([near_in_ref[b, :, at], stack[:, at]], axis=0)
            mixed = jnp.dot(matrix, both, preferred_element_type=F32)
            done[b, :, :, at] = ((part_ref[b, :, at] + mixed).astype(BF) * live).reshape(c, 2, wide)
            if w % 2:
                lanes = pl.ds((w - 1) * wide, 2 * wide)
                copies.append(pltpu.make_async_copy(done.at[b, :, :, lanes], out_ref.at[0, b, :, :, lanes],
                                                    sems.at[len(copies)]))
                copies[-1].start()
    for copy in copies:
        copy.wait()


def final(live, weight, matrix, plane, part, note, near_in):
    s, c, n = near_in.shape
    return pl.pallas_call(
        final_kernel, name="final",
        in_specs=[SM] + [VM] * 6, out_specs=HB,
        out_shape=jax.ShapeDtypeStruct((1, s, c, 2, n), BF),
        scratch_shapes=[pltpu.VMEM((c, n), BF), pltpu.VMEM((s, c, 2, n), BF),
                        pltpu.VMEM((s, 3, c, LANES), F32), pltpu.VMEM((s, 3, c, LANES), F32),
                        pltpu.SemaphoreType.DMA((n // 1024 * SLOTS,))],
        compiler_params=params(12), cost_estimate=cost(2),
    )(live, weight, matrix, plane, part, note, near_in)


def swap(value, axis, first):
    count = lax.axis_size(axis)
    pairs = []
    for i in range(first, count - 1, 2):
        pairs += [(i, i + 1), (i + 1, i)]
    return lax.ppermute(value, axis, pairs)


def ring(value, axis, steps):
    count = lax.axis_size(axis)
    return lax.ppermute(value, axis, [(i, (i + steps) % count) for i in range(count)])


def body(volume, tissue, face_owner, face_slot, plane_weight, depth_weight, norm_gain, norm_bias):
    owner = jnp.transpose(face_owner, (0, 2, 3, 1))
    slot = jnp.transpose(face_slot, (0, 2, 1))
    gain = norm_gain.reshape(1, -1)
    bias = norm_bias.reshape(1, -1)
    me = lax.axis_index("blk").reshape(1)
    side = (lax.axis_index("slab") % 2).reshape(1)
    near, far, strips, kept = split(side, me, volume, tissue)
    raw = swap(far, "slab", 1)
    one, three, two = (ring(strips, "blk", k) for k in (1, 3, 2))
    strips = [strips, one, three, two]
    plane, found, taps = bulk(plane_weight, near, far)
    note, edge, norm = stats(me, tissue, owner, slot, taps, gain, bias, found, strips)
    note_in = swap(note, "slab", 1)
    near_act = near_layer(plane, edge, norm)
    near_in = swap(near_act, "slab", 0)
    far_plane, part, matrix = inner(side, taps, depth_weight, kept, raw, near_act, plane, edge, norm)
    return final(tissue, taps, matrix, far_plane, part, note_in, near_in)


def solution(mesh):
    return jax.shard_map(
        body,
        mesh=mesh,
        in_specs=(
            P("slab", "blk", None, None, None),
            P("slab", "blk"),
            P(None, "blk", None, None),
            P(None, "blk", None),
            P(),
            P(),
            P(),
            P(),
        ),
        out_specs=P("slab", "blk", None, None, None),
        check_vma=False,
    )
```
